128 devices in a mesh: dp: 2 (over z_hi), fsdp: 8 (over z_lo, y), seq: 8 (over x, core).
Axes of the slice: x: 4, y: 4, z: 4 (z_hi: 2, z_lo: 2; z = z_hi * 2 + z_lo), core: 2. Of those that a mesh axis runs over, the one named last changes fastest.
Arguments:
- tokens: bfloat16 [512, 200, 512], P(('dp', 'fsdp', 'seq')), may hold values from -6 to 6
- key_mask: int32 [512, 200], P(('dp', 'fsdp', 'seq')), may hold values from 0 to 1, as said below
- image_live: int32 [512], P(('dp', 'fsdp', 'seq')), may hold values 0 or 1
- routes: int32 [512, 200, 2], P(('dp', 'fsdp', 'seq')), may hold values from 0 to 3, all different within a row; in each aligned block of 800 rows (0 to 799, 800 to 1599, ..., all dimensions but the last counted through in order) at most 600 rows name the same one
- ln1_gain: bfloat16 [512], P('fsdp'), may hold values from 0.5 to 1.5
- ln1_bias: bfloat16 [512], P('fsdp'), may hold values from -3 to 3
- w_qkv: bfloat16 [512, 1536], P('fsdp'), may hold values from -0.25 to 0.25
- w_attn: bfloat16 [512, 512], P('fsdp'), may hold values from -1 to 1
- ln2_gain: bfloat16 [512], P('fsdp'), may hold values from 0.5 to 1.5
- ln2_bias: bfloat16 [512], P('fsdp'), may hold values from -3 to 3
- w_router: bfloat16 [512, 4], P('fsdp'), may hold values from -0.1796875 to 0.1796875
- w_in: bfloat16 [4, 512, 2048], P(None, None, 'fsdp'), may hold values from -0.25 to 0.25
- w_out: bfloat16 [4, 2048, 512], P(None, 'fsdp'), may hold values from -0.25 to 0.25
- cotangent: bfloat16 [512, 200, 512], P(('dp', 'fsdp', 'seq')), may hold values from -6 to 6
Outputs:
- layer_out: bfloat16 [512, 200, 512], P(('dp', 'fsdp', 'seq'))
- grad_tokens: float32 [512, 200, 512], P(('dp', 'fsdp', 'seq'))
- grad_ln1_gain: float32 [512], P('fsdp')
- grad_ln1_bias: float32 [512], P('fsdp')
- grad_w_qkv: float32 [512, 1536], P('fsdp')
- grad_w_attn: float32 [512, 512], P('fsdp')
- grad_ln2_gain: float32 [512], P('fsdp')
- grad_ln2_bias: float32 [512], P('fsdp')
- grad_w_router: float32 [512, 4], P('fsdp')
- grad_w_in: float32 [4, 512, 2048], P(None, None, 'fsdp')
- grad_w_out: float32 [4, 2048, 512], P(None, 'fsdp')
The draws below stay inside these ranges and needn't reach their ends.
Inputs may be any that keep to these rules, and one draw needn't show every extreme that they name: `key_mask`: position 0 of every image slot is 1. `routes`: among the token slots of one device (800 in a row, aligned), no expert is named by more than 600 tokens, a bound that some block reaches.
All inputs are finite; a program needn't handle non-finite values. No bound on the sum of `image_live` on one device may be relied on, other than what follows from the above.
Results may differ from the reference program's by a relative error of at most 0.029.
Values may be sent and summed in bfloat16 or wider, within the bound.
A program may use at most 192 MiB of HBM per device.

```python
import math
import jax
import jax.numpy as jnp
import numpy as np
from jax import lax

D = 512
HEADS = 8
FF = 2048
EXPERTS = 4
TOPK = 2
LEN = 200
IMG_DEV = 4
CAP = 600
IMAGES = 512


def draw_key_mask(key, part):
    key = jax.random.fold_in(key, 5)
    picks = jax.random.randint(key, (IMAGES, LEN), 0, 10)
    valid = (picks < 9).astype(jnp.int32)
    first = lax.broadcasted_iota(jnp.int32, (IMAGES, LEN), 1) == 0
    return jnp.where(first, 1, valid).astype(jnp.int32)


def plant(values, own_key, low, top_value):
    longest = values.shape.index(max(values.shape))
    spots = []
    for shift in (0, 1):
        where = [jax.random.randint(jax.random.fold_in(own_key, axis), (), 0, length) for axis, length in enumerate(values.shape)]
        where[longest] = (where[longest] + shift) % values.shape[longest]
        spots.append(tuple(where))
    return values.at[spots[0]].set(low).at[spots[1]].set(top_value)


def level_of(rng, dims, shards, low, high):
    def one(position, parts):
        steps = jax.random.uniform(jax.random.fold_in(jax.random.fold_in(rng, 6), position), (parts,), jnp.float32, low / len(shards), high / len(shards))
        return jnp.repeat(jnp.exp(steps), dims[position] // parts).reshape((-1,) + (1,) * (len(dims) - position - 1))

    factor_of = one(*shards[0])
    for cut in shards[1:]:
        factor_of = factor_of * one(*cut)
    return factor_of


def routed_block(own_key, own, number, rows, amount, top, limit, skew):
    ranking = jax.random.permutation(own_key, amount)
    crowded, common = shares(amount, rows * top, limit, skew, True), shares(amount, rows * top, limit, skew, False)
    places = jnp.arange(amount)

    def named(sizes, rotation):
        used = int((sizes > 0).sum())
        fixed = max(1, used // 4)
        moved = fixed + (places - fixed + rotation * (used - fixed)) % max(1, amount - fixed)
        return jnp.zeros((amount,), jnp.int32).at[ranking[jnp.where(places < fixed, places, moved)]].set(jnp.asarray(sizes, jnp.int32))

    sizes = jnp.where(number % 4 == 0, named(crowded, number // 4), named(common, number - number // 4 - 1))
    mixed = jax.random.permutation(jax.random.fold_in(own, 3), amount)
    giver, receiver = mixed[0:amount // 2 * 2:2], mixed[1:amount // 2 * 2:2]
    margin = jnp.minimum(sizes[giver] - 1, limit - sizes[receiver]) // 2
    margin = jnp.where((giver == ranking[0]) | (receiver == ranking[0]) | (sizes[receiver] == 0), 0, jnp.maximum(margin, 0))
    moved = jax.random.randint(jax.random.fold_in(own, 4), (amount // 2,), 0, 1 << 20) % (margin + 1)
    sizes = sizes.at[giver].add(-moved).at[receiver].add(moved)
    members = jnp.searchsorted(jnp.cumsum(sizes), jnp.arange(rows * top), side="right").astype(jnp.int32)
    table = members.reshape(top, rows).T
    table = table[jax.random.permutation(jax.random.fold_in(own, 1), rows)]
    rotation = jax.random.randint(jax.random.fold_in(own, 2), (rows, 1), 0, top)
    return jnp.take_along_axis(table, (jnp.arange(top)[None, :] + rotation) % top, axis=1)


def shares(count, total, limit, lean, full):
    weights = [(1 << 20) // math.isqrt(standing ** lean) + 1 for standing in range(1, count + 1)]
    largest = limit if full else min(limit, max(-(-total // count), total * weights[0] // sum(weights)))
    least = 1 if total - largest >= count - 1 else 0
    given, rest = [largest] + [least] * (count - 1), total - largest - least * (count - 1)
    while rest > 0:
        movable = [i for i in range(1, count) if given[i] < largest] or [i for i in range(1, count) if given[i] < limit]
        pool, budget = sum([weights[i] for i in movable]), rest
        for i in movable:
            extra = min(limit - given[i], max(1, budget * weights[i] // pool), rest)
            given[i] = given[i] + extra
            rest = rest - extra
    return np.array(given)


def scatter_about(stream_key, extent, width, bound, shards=(), held_as=jnp.bfloat16):
    level = level_of(stream_key, extent, shards, -0.22, 0.18) if shards else 1.0
    values = jax.random.normal(stream_key, extent, jnp.float32) * width * level
    return jnp.minimum(jnp.maximum(values, -bound), bound).astype(held_as)


def setup_inputs(seed: int = 0) -> dict:
    splits = jax.random.split(jax.random.key(seed), 15)
    tokens = scatter_about(splits[0], (IMAGES, LEN, D), 1.0, 6.0, ((0, 128),))
    key_mask = draw_key_mask(jax.random.fold_in(splits[14], 71), 0)
    image_live = plant((jax.random.randint(splits[2], (IMAGES,), 0, 4) < 3).astype(jnp.int32), jax.random.fold_in(splits[2], 1), 0, 1)
    routes_keys = jax.random.split(jax.random.fold_in(splits[3], 1), IMAGES * LEN // (IMG_DEV * LEN))
    routes_turns = jax.random.permutation(jax.random.fold_in(splits[3], 3), IMAGES * LEN // (IMG_DEV * LEN))
    routes = jax.vmap(lambda own, number: routed_block(jax.random.fold_in(splits[3], 2), own, number, IMG_DEV * LEN, EXPERTS, TOPK, CAP, 1))(routes_keys, routes_turns).reshape((IMAGES, LEN, TOPK))
    ln1_gain = jnp.clip(1.0 + 0.1 * jax.random.normal(splits[4], (D,), jnp.float32), 0.5, 1.5).astype(jnp.bfloat16)
    ln1_bias = scatter_about(splits[5], (D,), 0.3, 3.0, ((0, 8),))
    w_qkv = scatter_about(splits[6], (D, 3 * D), D ** -0.5, 0.25, ((0, 8),))
    w_attn = scatter_about(splits[7], (D, D), (D // 16) ** -0.5, 1.0, ((0, 8),))
    ln2_gain = jnp.clip(1.0 + 0.1 * jax.random.normal(splits[8], (D,), jnp.float32), 0.5, 1.5).astype(jnp.bfloat16)
    ln2_bias = scatter_about(splits[9], (D,), 0.3, 3.0, ((0, 8),))
    w_router = scatter_about(splits[10], (D, EXPERTS), 0.03, 0.1796875, ((0, 8),))
    w_in = scatter_about(splits[11], (EXPERTS, D, FF), D ** -0.5, 0.25, ((2, 8),))
    w_out = scatter_about(splits[12], (EXPERTS, FF, D), (FF // 4) ** -0.5, 0.25, ((1, 8),))
    cotangent = scatter_about(splits[13], (IMAGES, LEN, D), 1.0, 6.0, ((0, 128),))
    return {"tokens": tokens, "key_mask": key_mask, "image_live": image_live, "routes": routes, "ln1_gain": ln1_gain, "ln1_bias": ln1_bias, "w_qkv": w_qkv, "w_attn": w_attn, "ln2_gain": ln2_gain, "ln2_bias": ln2_bias, "w_router": w_router, "w_in": w_in, "w_out": w_out, "cotangent": cotangent}


EPS = 1e-06
NEG_FILL = -1000000000.0
HIGH = lax.Precision.HIGHEST

@jax.custom_vjp
def low(v):
    return lax.optimization_barrier(v.astype(jnp.bfloat16)).astype(jnp.float32)

@jax.custom_vjp
def low_back(v):
    return v

def low_keep(v):
    return (low(v), None)

def low_pass(kept, grad):
    return (grad,)

def back_keep(v):
    return (v, None)

def back_low(kept, grad):
    return (low(grad),)
low.defvjp(low_keep, low_pass)
low_back.defvjp(back_keep, back_low)

def layer_norm(values, gain, shift):
    center = values - lax.optimization_barrier(jnp.mean(values, axis=-1, keepdims=True))
    spread = lax.optimization_barrier(jnp.mean(center * center, axis=-1, keepdims=True))
    return center * lax.rsqrt(spread + EPS) * gain + shift

def image_layer(inputs, key_valid, live_flag, route_ids, params):
    gain_one, shift_one, qkv_weight, attn_weight, gain_two, shift_two, router_weight, in_weight, out_weight = params
    head_dim = D // HEADS
    normed = low(layer_norm(inputs, gain_one, shift_one))
    packed = low_back(low(jnp.dot(normed, qkv_weight, precision=HIGH)))
    packed = packed.reshape(LEN, 3, HEADS, head_dim)
    queries = packed[:, 0]
    keys_all = packed[:, 1]
    values = packed[:, 2]
    scores = low_back(jnp.einsum('qhd,khd->hqk', queries, keys_all, precision=HIGH)) * head_dim ** (-0.5)
    scores = jnp.where(key_valid[None, None, :] > 0, scores, NEG_FILL)
    weights = low(jax.nn.softmax(scores, axis=-1))
    attended = low_back(low(jnp.einsum('hqk,khd->qhd', weights, values, precision=HIGH))).reshape(LEN, D)
    branch = low_back(jnp.dot(attended, attn_weight, precision=HIGH))
    middle = inputs + branch
    normed_two = low(layer_norm(middle, gain_two, shift_two))
    logits = jnp.dot(normed_two, router_weight, precision=HIGH)
    gates = jax.nn.softmax(logits, axis=-1)
    chosen = lax.optimization_barrier(jnp.sum(jax.nn.one_hot(route_ids, EXPERTS, dtype=gates.dtype), axis=1))
    combine = low(gates * chosen)
    hidden = low_back(jnp.einsum('ld,edf->elf', normed_two, in_weight, precision=HIGH))
    active = low(jax.nn.gelu(hidden, approximate=False))
    expert_out = low_back(jnp.einsum('elf,efd->eld', active, out_weight, precision=HIGH))
    mixed = low_back(jnp.einsum('le,eld->ld', combine, expert_out, precision=HIGH))
    return jnp.where(live_flag > 0, middle + mixed, inputs)

def reference(tokens, key_mask, image_live, routes, ln1_gain, ln1_bias, w_qkv, w_attn, ln2_gain, ln2_bias, w_router, w_in, w_out, cotangent):
    params = tuple((weight.astype(jnp.float32) for weight in (ln1_gain, ln1_bias, w_qkv, w_attn, ln2_gain, ln2_bias, w_router, w_in, w_out)))

    def one_image(totals, item):
        image, valid, live_flag, route_ids, grad_out = item

        def forward(inputs, weights):
            return image_layer(inputs, valid, live_flag, route_ids, weights)
        result, pull = jax.vjp(forward, image.astype(jnp.float32), params)
        grad_image, grad_params = pull(grad_out.astype(jnp.float32))
        totals = jax.tree.map(jnp.add, totals, grad_params)
        return (totals, (result.astype(jnp.bfloat16), grad_image))
    zeros = tuple((jnp.zeros_like(weight) for weight in params))
    totals, (results, grads) = lax.scan(one_image, zeros, (tokens, key_mask, image_live, routes, cotangent))
    return (results, grads) + tuple(totals)
```

```python
import jax
import jax.numpy as jnp
from jax import lax
from jax.sharding import PartitionSpec as P

HEADS = 8
EPS = 1e-06
NEG_FILL = -1000000000.0
HIGH = lax.Precision.HIGHEST
F32 = jnp.float32
BF16 = jnp.bfloat16


def normalize(values):
    center = values - jnp.mean(values, axis=-1, keepdims=True)
    scale_inv = lax.rsqrt(jnp.mean(center * center, axis=-1, keepdims=True) + EPS)
    return (center * scale_inv, scale_inv)


def norm_back(grad_out, normed, scale_inv, gain):
    scaled = grad_out * gain
    inner = (
        scaled
        - jnp.mean(scaled, axis=-1, keepdims=True)
        - normed * jnp.mean(scaled * normed, axis=-1, keepdims=True)
    )
    return (scale_inv * inner, jnp.sum(grad_out * normed, axis=0), jnp.sum(grad_out, axis=0))


def dot(a, b):
    return jnp.dot(a, b, preferred_element_type=F32)


def ein(spec, a, b):
    return jnp.einsum(spec, a, b, preferred_element_type=F32)


def per_device(
    tokens, key_mask, image_live, routes, ln1_gain, ln1_bias, w_qkv, w_attn, ln2_gain, ln2_bias,
    w_router, w_in, w_out, cotangent,
):
    images, length, width = tokens.shape
    rows = images * length
    experts = w_in.shape[0]
    hd = width // HEADS
    scale = hd ** (-0.5)

    def gather(v, axis):
        return lax.all_gather(v, "fsdp", axis=axis, tiled=True)

    small = jnp.concatenate(
        [w_qkv, w_attn, w_router, ln1_gain[:, None], ln1_bias[:, None], ln2_gain[:, None], ln2_bias[:, None]], axis=1
    )
    small = gather(small, 0)
    q3 = 3 * width
    qkv_full = small[:, :q3]
    attn_full = small[:, q3 : q3 + width]
    router_full = small[:, q3 + width : q3 + width + experts]
    vecs = small[:, q3 + width + experts :].astype(F32)
    gain_one, shift_one, gain_two, shift_two = (vecs[:, i] for i in range(4))
    in_full = gather(w_in, 2)
    out_full = gather(w_out, 1)

    inputs = tokens.reshape(rows, width).astype(F32)
    normed_one, inv_one = normalize(inputs)
    block_one = (normed_one * gain_one + shift_one).astype(BF16)
    packed = dot(block_one, qkv_full).astype(BF16).reshape(images, length, 3, HEADS, hd)
    queries, keys_all, values = packed[:, :, 0], packed[:, :, 1], packed[:, :, 2]
    scores = ein("gqhd,gkhd->ghqk", queries, keys_all) * scale
    scores = jnp.where((key_mask > 0)[:, None, None, :], scores, NEG_FILL)
    top = jnp.max(scores, axis=-1, keepdims=True)
    expo = jnp.exp(scores - top)
    probs = expo / jnp.sum(expo, axis=-1, keepdims=True)
    probs_low = probs.astype(BF16)
    attended = ein("ghqk,gkhd->gqhd", probs_low, values).astype(BF16).reshape(rows, width)
    middle = inputs + dot(attended, attn_full)
    normed_mid, inv_two = normalize(middle)
    h2 = (normed_mid * gain_two + shift_two).astype(BF16)
    gates = jax.nn.softmax(dot(h2, router_full), axis=-1)
    route_rows = routes.reshape(rows, routes.shape[-1])
    chosen = jnp.sum(
        (route_rows[:, :, None] == jnp.arange(experts, dtype=jnp.int32)[None, None, :]).astype(F32), axis=1
    )
    comb = (gates * chosen).astype(BF16).astype(F32)

    live_rows = jnp.broadcast_to(image_live[:, None] > 0, (images, length)).reshape(rows, 1)
    grad_in = cotangent.reshape(rows, width).astype(F32)
    grad_live = jnp.where(live_rows, grad_in, 0.0)
    gm = grad_live.astype(BF16)

    hid = ein("rd,edf->erf", h2, in_full)
    ga = ein("rd,efd->erf", gm, out_full)
    cdf = 0.5 * (1.0 + lax.erf(hid * 0.7071067811865476))
    slope = cdf + hid * jnp.exp(-0.5 * hid * hid) * 0.3989422804014327
    act = hid * cdf
    comb_e = comb.T[:, :, None]
    gc = jnp.sum(act * ga, axis=-1).T
    cact = (act * comb_e).astype(BF16)
    ghid = (ga * comb_e * slope).astype(BF16)
    mixed = ein("erf,efd->rd", cact, out_full)
    grad_out_w = ein("erf,rd->efd", cact, gm)
    grad_in_w = ein("rd,erf->edf", h2, ghid)
    gh2 = ein("erf,edf->rd", ghid, in_full)
    layer_out = jnp.where(live_rows, middle + mixed, inputs).astype(BF16).reshape(images, length, width)

    gg = gc * chosen
    glog = gates * (gg - jnp.sum(gg * gates, axis=-1, keepdims=True))
    grad_router = jnp.dot(h2.astype(F32).T, glog, precision=HIGH)
    gh2 = gh2 + jnp.dot(glog, router_full.astype(F32).T, precision=HIGH)
    gmid, gg2, gs2 = norm_back(gh2, normed_mid, inv_two, gain_two)
    grad_middle = grad_live + gmid
    gal = grad_middle.astype(BF16)
    grad_attn_w = ein("rd,re->de", attended, gal)
    go = ein("re,de->rd", gal, attn_full).astype(BF16).reshape(images, length, HEADS, hd)
    gp = ein("gqhd,gkhd->ghqk", go, values)
    gs = (probs * (gp - jnp.sum(gp * probs, axis=-1, keepdims=True)) * scale).astype(BF16)
    gq = ein("ghqk,gkhd->gqhd", gs, keys_all)
    gk = ein("ghqk,gqhd->gkhd", gs, queries)
    gv = ein("ghqk,gqhd->gkhd", probs_low, go)
    gpacked = jnp.stack([gq, gk, gv], axis=2).astype(BF16).reshape(rows, 3 * width)
    grad_qkv_w = ein("rd,re->de", block_one, gpacked)
    gh1 = ein("re,de->rd", gpacked, qkv_full)
    gin, gg1, gs1 = norm_back(gh1, normed_one, inv_one, gain_one)
    grad_tokens = (jnp.where(live_rows, 0.0, grad_in) + grad_middle + gin).reshape(images, length, width)

    def reduce(v, axis):
        v = lax.psum_scatter(v.astype(BF16), "fsdp", scatter_dimension=axis, tiled=True)
        return lax.psum(v, ("dp", "seq")).astype(F32)

    gsmall = jnp.concatenate(
        [grad_qkv_w, grad_attn_w, grad_router, gg1[:, None], gs1[:, None], gg2[:, None], gs2[:, None]], axis=1
    )
    gsmall = reduce(gsmall, 0)
    g_in = reduce(grad_in_w, 2)
    g_out = reduce(grad_out_w, 1)
    r = q3 + width + experts
    return (
        layer_out,
        grad_tokens,
        gsmall[:, r],
        gsmall[:, r + 1],
        gsmall[:, :q3],
        gsmall[:, q3 : q3 + width],
        gsmall[:, r + 2],
        gsmall[:, r + 3],
        gsmall[:, q3 + width : r],
        g_in,
        g_out,
    )


def solution(mesh):
    dev = ("dp", "fsdp", "seq")
    in_specs = (
        P(dev, None, None), P(dev, None), P(dev), P(dev, None, None), P("fsdp"), P("fsdp"), P("fsdp", None),
        P("fsdp", None), P("fsdp"), P("fsdp"), P("fsdp", None), P(None, None, "fsdp"), P(None, "fsdp", None),
        P(dev, None, None),
    )
    out_specs = (
        P(dev, None, None), P(dev, None, None), P("fsdp"), P("fsdp"), P("fsdp", None), P("fsdp", None), P("fsdp"),
        P("fsdp"), P("fsdp", None), P(None, None, "fsdp"), P(None, "fsdp", None),
    )
    return jax.shard_map(per_device, mesh=mesh, in_specs=in_specs, out_specs=out_specs, check_vma=False)
```

```python
import jax
import jax.numpy as jnp
from jax import lax
from jax.experimental import pallas as pl
from jax.experimental.pallas import tpu as pltpu
from jax.sharding import PartitionSpec as P

F32 = jnp.float32
BF16 = jnp.bfloat16
MESH = pl.DeviceIdType.MESH
HEADS = 8
EPS = 1e-06
NEG = -1000000000.0
D = 512
IMG = 4
LEN = 200
PAD = 208
ROWS = IMG * PAD
PAIR = 2 * ROWS
HD = 64
CH = 512
TM = 832
RA, RB, RC = 64, 32, 32


def dot(a, b):
    return jnp.dot(a, b, preferred_element_type=F32)


def dot_nt(a, b):
    return lax.dot_general(a, b, (((1,), (1,)), ((), ())), preferred_element_type=F32)


def dot_tn(a, b):
    return lax.dot_general(a, b, (((0,), (0,)), ((), ())), preferred_element_type=F32)


def rows_of(i):
    return pl.ds(pl.multiple_of(i * PAD, 16), PAD)


def span(start, size, unit):
    return pl.ds(pl.multiple_of(start, unit), size)


def pad_rows(v):
    return jnp.concatenate([v, jnp.zeros((PAD - LEN, v.shape[1]), v.dtype)], axis=0)


def normalize(v):
    c = v - jnp.mean(v, axis=-1, keepdims=True)
    r = lax.rsqrt(jnp.mean(c * c, axis=-1, keepdims=True) + EPS)
    return c * r, r


def lane(shape):
    return lax.broadcasted_iota(jnp.int32, shape, 1)


def loop(lo, hi, body):
    def step(i, carry):
        body(i)
        return carry

    lax.fori_loop(lo, hi, step, 0)


def norm_back(u, n, r):
    return r * (u - jnp.mean(u, axis=-1, keepdims=True) - n * jnp.mean(u * n, axis=-1, keepdims=True))


def ln_one(tok, mt, h1):
    def body(i):
        n, _ = normalize(pad_rows(tok[i].astype(F32)))
        h1[rows_of(i)] = (n * mt[4:5] + mt[5:6]).astype(BF16)

    loop(0, IMG, body)


def make_qkv(s_ref, h1, qkv):
    for b in range(3):
        v = dot(h1[...], s_ref[:, D * b : D * b + D]).astype(BF16)
        if b == 0:
            v = v * jnp.asarray(HD**-0.5, BF16)
        qkv[:, D * b : D * b + D] = v


def attend(i, qkv, kb, pb, ob):
    r = rows_of(i)
    bias = kb[i]
    low = lane((PAD, 128)) < HD
    for hp in range(HEADS // 2):
        o = 128 * hp
        q2, k2, v2 = qkv[r, o : o + 128], qkv[r, D + o : D + o + 128], qkv[r, 2 * D + o : 2 * D + o + 128]
        outs = []
        for a in range(2):
            qm = jnp.where(low if a == 0 else ~low, q2, jnp.zeros_like(q2))
            s = dot_nt(qm, k2) + bias
            e = jnp.exp(s - jnp.max(s, axis=-1, keepdims=True))
            p = (e * (1.0 / jnp.sum(e, axis=-1, keepdims=True))).astype(BF16)
            pb[i * HEADS + hp * 2 + a] = p
            outs.append(dot(p, v2))
        ob[r, o : o + 128] = jnp.where(low, outs[0], outs[1]).astype(BF16)


def middle(i, tok, s_ref, mt, ob, aux, x1, h2, gates, comb):
    r = rows_of(i)
    v = pad_rows(tok[i].astype(F32)) + dot(ob[r], s_ref[:, 1536:2048])
    x1[r] = v
    n, _ = normalize(v)
    h = (n * mt[6:7] + mt[7:8]).astype(BF16)
    h2[r] = h
    lg = dot(h, s_ref[:, 2048:2176])
    ok = lane((PAD, 128)) < 4
    lg = jnp.where(ok, lg, -1e30)
    e = jnp.exp(lg - jnp.max(lg, axis=-1, keepdims=True))
    g = e / jnp.sum(e, axis=-1, keepdims=True)
    gates[r] = g
    comb[r] = jnp.where(ok, g * aux[r].astype(F32), 0.0).astype(BF16)


def live_cotangent(i, cot, aux, gm):
    r = rows_of(i)
    gm[r] = (pad_rows(cot[i].astype(F32)) * aux[r, 4:5].astype(F32)).astype(BF16)


def expander():
    return (
        lax.broadcasted_iota(jnp.int32, (128, CH), 0) == lax.broadcasted_iota(jnp.int32, (128, CH), 1) // 128
    ).astype(BF16)


def experts_tile(lo, w, h2, gm, cx, gca, m, gh2, cag):
    r = pl.ds(lo, TM)
    win, wout = w[:CH], w[CH:]
    hid = dot(h2[r], win)
    ga = dot_nt(gm[r], wout)
    cdf = 0.5 * (1.0 + lax.erf(hid * 0.7071067811865476))
    slope = cdf + hid * jnp.exp(-0.5 * hid * hid) * 0.3989422804014327
    act = hid * cdf
    c = cx[r].astype(F32)
    gca[r] += act * ga
    ca = (act * c).astype(BF16)
    gh = (ga * c * slope).astype(BF16)
    cag[r, :CH] = ca
    cag[r, CH:] = gh
    m[r] += dot(ca, wout)
    gh2[r] += dot_nt(gh, win)


def layer_result(i, tok, aux, x1, m, mr, out):
    r = rows_of(i)
    v = x1[r] + m[r] + mr[r].astype(F32)
    out[i] = jnp.where(aux[r, 4:5].astype(F32) > 0, v, pad_rows(tok[i].astype(F32)))[:LEN].astype(BF16)


def second_norm_back(i, s_ref, mt, aux, gates, gca, gcr, gh2, gh2r, gm, x1, glb, gab, vec):
    r = rows_of(i)
    ok = lane((PAD, 128)) < 4
    ch = jnp.where(ok, aux[r].astype(F32), 0.0)
    g = gates[r]
    gg = (dot_nt(gca[r].astype(BF16), expander()) + gcr[r]) * ch
    gl = (g * (gg - jnp.sum(gg * g, axis=-1, keepdims=True))).astype(BF16)
    glb[r] = gl
    gh = gh2[r] + gh2r[r].astype(F32) + dot_nt(gl, s_ref[:, 2048:2176])
    n, r2 = normalize(x1[r])
    vec[6:7] += jnp.sum(gh * n, axis=0, keepdims=True)
    vec[7:8] += jnp.sum(gh, axis=0, keepdims=True)
    gx = gm[r].astype(F32) + norm_back(gh * mt[6:7], n, r2)
    x1[r] = gx
    gab[r] = gx.astype(BF16)


def attend_back(i, qkv, pb, cag):
    r = rows_of(i)
    rv = span(ROWS + i * PAD, PAD, 16)
    low = lane((PAD, 128)) < HD
    for hp in range(HEADS // 2):
        o = 128 * hp
        q2, k2, v2 = qkv[r, o : o + 128], qkv[r, D + o : D + o + 128], qkv[r, 2 * D + o : 2 * D + o + 128]
        g2 = cag[rv, D + o : D + o + 128]
        gq, gk, gv = [], [], []
        for a in range(2):
            gmk = jnp.where(low if a == 0 else ~low, g2, jnp.zeros_like(g2))
            p = pb[i * HEADS + hp * 2 + a]
            pf = p.astype(F32)
            t = dot_nt(gmk, v2)
            gs = (pf * (t - jnp.sum(t * pf, axis=-1, keepdims=True))).astype(BF16)
            gq.append(dot(gs, k2))
            gk.append(dot_tn(gs, q2))
            gv.append(dot_tn(p, g2))
        cag[r, o : o + 128] = (jnp.where(low, gq[0], gq[1]) * HD**-0.5).astype(BF16)
        cag[r, D + o : D + o + 128] = jnp.where(low, gk[0], gk[1]).astype(BF16)
        cag[rv, o : o + 128] = jnp.where(low, gv[0], gv[1]).astype(BF16)


def first_norm_back(i, tok, cot, aux, s_ref, mt, cag, x1, vec, gt):
    r = rows_of(i)
    rv = span(ROWS + i * PAD, PAD, 16)
    gh = (
        dot_nt(cag[r, :D], s_ref[:, :D])
        + dot_nt(cag[r, D:], s_ref[:, D : 2 * D])
        + dot_nt(cag[rv, :D], s_ref[:, 2 * D : 3 * D])
    )
    n, r1 = normalize(pad_rows(tok[i].astype(F32)))
    vec[4:5] += jnp.sum(gh * n, axis=0, keepdims=True)
    vec[5:6] += jnp.sum(gh, axis=0, keepdims=True)
    gd = jnp.where(aux[r, 4:5].astype(F32) > 0, 0.0, pad_rows(cot[i].astype(F32)))
    gt[i] = (gd + x1[r] + norm_back(gh * mt[4:5], n, r1))[:LEN]


def order(k):
    dy = jnp.where((k == 2) | (k == 5), 1, jnp.where((k == 3) | (k == 6), 3, jnp.where((k == 4) | (k == 7), 2, 0)))
    dz = jnp.where((k == 1) | (k >= 5), 1, 0)
    return dz, dy


def kernel(
    tok, kb, aux, cot, s_in, w_in, w_out,
    out, gt, sf, misc, w_all, f_all, r1a, r1b, r1c,
    s_ref, wbuf, gst, h1, h1t, qkv, pb, ob, x1, h2, gm, h2t, gmt, gates, comb, cx, m, gh2, gca, cag,
    gh2r, mr, gcp, gcr, mt, vec, mx,
    cr, gc, qa1, qb1, qa2, qb2, qa3, qb3, ga2, gb2, ga3, gb3, r2a, r2b, r2c,
    r3a, r3b, r3c,
    lsem, sy, sz, sc, wy, wz, px, ssem, lsem2, rsem, asem, gsem, msem, wsem,
):
    zh, f, sq = lax.axis_index("dp"), lax.axis_index("fsdp"), lax.axis_index("seq")
    zl, y = f // 4, f % 4
    x, c = sq // 2, sq % 2
    z = zh * 2 + zl

    def dev(zh_=zh, zl_=zl, y_=y, x_=x, c_=c):
        return (zh_, zl_ * 4 + y_, x_ * 2 + c_)

    def up(v, d):
        return (v + d) % 4

    def dev_z(zz):
        return dev(zh_=zz // 2, zl_=zz % 2)

    core = dev(c_=1 - c)

    def rdma(src, dst, ssm, rsm, target):
        return pltpu.make_async_remote_copy(
            src_ref=src, dst_ref=dst, send_sem=ssm, recv_sem=rsm, device_id=target, device_id_type=MESH
        )

    barrier = pltpu.get_barrier_semaphore()
    for d in (1, 2, 3):
        for target in (dev(x_=up(x, d)), dev(y_=up(y, d)), dev_z(up(z, d))):
            pl.semaphore_signal(barrier, inc=1, device_id=target, device_id_type=MESH)
    pl.semaphore_signal(barrier, inc=1, device_id=core, device_id_type=MESH)

    own = [pltpu.make_async_copy(s_in, s_ref.at[span(64 * f, 64, 64)], lsem.at[0])]
    half = span(128 * c, 128, 128)
    for e in range(4):
        own.append(
            pltpu.make_async_copy(w_in.at[e, :, half], w_all.at[f, :CH, 128 * e : 128 * e + 128], lsem.at[1 + e])
        )
        own.append(
            pltpu.make_async_copy(w_out.at[e, half, :], w_all.at[f, CH + 128 * e : CH + 128 * e + 128], lsem.at[5 + e])
        )
    for cp in own:
        cp.start()
    pl.semaphore_wait(barrier, 10)
    own[0].wait()

    def s_rows(zz, yy, size=32, off=0):
        return s_ref.at[span((zz * 4 + yy) * 64 + 32 * c + off, size, 16)]

    def s_y(d):
        r = s_rows(zl, y)
        return rdma(r, r, sy.at[0, d], sy.at[1, d], dev(y_=up(y, d)))

    def s_z(way, d):
        r = s_rows(zl, up(y, 4 - d), 16, 16 * way)
        return rdma(r, r, sz.at[0, way, d], sz.at[1, way, d], dev_z(up(z, 1 if way == 0 else 3)))

    def s_c(dz, d):
        r = s_rows((zl + dz) % 2, up(y, 4 - d))
        return rdma(r, r, sc.at[0, dz, d], sc.at[1, dz, d], core)

    def s_z_in(way, d):
        r = s_rows(1 - zl, up(y, 4 - d), 16, 16 * way)
        return rdma(r, r, sz.at[0, way, d], sz.at[1, way, d], dev_z(up(z, 1 if way == 0 else 3)))

    def s_y_in(d):
        r = s_rows(zl, up(y, 4 - d))
        return rdma(r, r, sy.at[0, d], sy.at[1, d], dev(y_=up(y, d)))

    def s_c_in(dz, d):
        r = s_ref.at[span((((zl + dz) % 2) * 4 + up(y, 4 - d)) * 64 + 32 * (1 - c), 32, 16)]
        return rdma(r, r, sc.at[0, dz, d], sc.at[1, dz, d], core)

    for d in (1, 3, 2):
        s_y(d).start()
    for way in (0, 1):
        s_z(way, 0).start()

    loop(0, IMG, lambda i: live_cotangent(i, cot, aux, gm))
    own_rows, peer_rows = pl.ds(0, ROWS), pl.ds(ROWS, ROWS)
    gm_x = rdma(gm.at[own_rows], gm.at[peer_rows], px.at[0, 0], px.at[1, 0], core)
    gm_x.start()

    for d in (1, 3, 2):
        s_y_in(d).wait_recv()
        for way in (0, 1):
            s_z(way, d).start()
        s_c(0, d).start()

    def w_y(d):
        return rdma(w_all.at[f], w_all.at[f], wy.at[0, d], wy.at[1, d], dev(y_=up(y, d)))

    def w_y_in(d):
        r = w_all.at[zl * 4 + up(y, 4 - d)]
        return rdma(r, r, wy.at[0, d], wy.at[1, d], dev(y_=up(y, d)))

    def w_half(zz, d, way):
        return w_all.at[zz * 4 + up(y, 4 - d), CH * way : CH * way + CH]

    def w_z(way, d, zz):
        r = w_half(zz, d, way)
        return rdma(r, r, wz.at[0, way, d], wz.at[1, way, d], dev_z(up(z, 1 if way == 0 else 3)))

    for cp in own[1:]:
        cp.wait()
    w_y(1).start()
    w_y(3).start()
    for way in (0, 1):
        w_z(way, 0, zl).start()

    gmt[:, :ROWS] = gm[:ROWS].T
    for d in (0, 1, 3, 2):
        for way in (0, 1):
            s_z_in(way, d).wait_recv()
        s_c(1, d).start()
    for dz in (0, 1):
        for d in range(4):
            if (dz, d) != (0, 0):
                s_c_in(dz, d).wait_recv()

    mt[...] = jnp.transpose(s_ref[:, 2048:2176].astype(F32))[:8]
    vec[...] = jnp.zeros_like(vec)
    ln_one(tok, mt, h1)
    make_qkv(s_ref, h1, qkv)
    w_y(2).start()

    def h2_x(i):
        return rdma(h2.at[rows_of(i)], h2.at[span(ROWS + i * PAD, PAD, 16)], px.at[0, 3 + i], px.at[1, 3 + i], core)

    def comb_x(i):
        return rdma(comb.at[rows_of(i)], comb.at[span(ROWS + i * PAD, PAD, 16)], px.at[0, 7 + i], px.at[1, 7 + i], core)

    def forward(i):
        attend(i, qkv, kb, pb, ob)
        middle(i, tok, s_ref, mt, ob, aux, x1, h2, gates, comb)
        h2_x(i).start()
        comb_x(i).start()

    loop(0, IMG, forward)
    gm_x.wait_recv()
    gmt[:, ROWS:] = gm[ROWS:].T
    h1t[...] = h1[...].T
    h2t[:, :ROWS] = h2[:ROWS].T

    def load_w(k):
        dz, dy = order(k)
        return pltpu.make_async_copy(w_all.at[((zl + dz) % 2) * 4 + up(y, 4 - dy)], wbuf.at[k % 2], wsem.at[k % 2])

    load_w(0).start()
    m[...] = jnp.zeros_like(m)
    gh2[...] = jnp.zeros_like(gh2)
    gca[...] = jnp.zeros_like(gca)
    ex = expander()
    cx[:ROWS] = dot(comb[:ROWS], ex).astype(BF16)
    loop(0, IMG, lambda i: (h2_x(i).wait_recv(), comb_x(i).wait_recv()))
    h2t[:, ROWS:] = h2[ROWS:].T
    cx[ROWS:] = dot(comb[ROWS:], ex).astype(BF16)

    def sends(k, act):
        slot = k % 2
        dz, dy = order(k)
        zz, yy = (zl + dz) % 2, up(y, 4 - dy)

        def local(src, dst, i):
            cp = pltpu.make_async_copy(src, dst, lsem2.at[slot, i])
            cp.start() if act == 0 else cp.wait()

        def remote(src, dst, i, rsm, target):
            cp = rdma(src, dst, ssem.at[slot, i], rsm, target)
            cp.start() if act == 0 else cp.wait_send()

        g = gst.at[slot]
        for d in (1, 2, 3):
            remote(g.at[:, up(x, d), :RA], r1a.at[d, zz, yy], d - 1, rsem.at[0, d], dev(x_=up(x, d)))
        local(g.at[:, x, :RA], r1a.at[0, zz, yy], 0)

        @pl.when(dy != 0)
        def _():
            remote(g.at[:, :, RA : RA + RB], r1b.at[dy, zz], 3, rsem.at[1, dy], dev(y_=yy))

        @pl.when(dy == 0)
        def _():
            local(g.at[:, :, RA : RA + RB], r1b.at[0, zz], 1)

        remote(g.at[1 - zh, :, RA + RB :], r1c.at[2 + dz, yy], 4, rsem.at[2, 2 + dz], dev(zh_=1 - zh, zl_=zz))

        @pl.when(dz != 0)
        def _():
            remote(g.at[zh, :, RA + RB :], r1c.at[1, yy], 5, rsem.at[2, 1], dev(zl_=zz))

        @pl.when(dz == 0)
        def _():
            local(g.at[zh, :, RA + RB :], r1c.at[0, yy], 2)

    gh2_x = rdma(cx.at[peer_rows], gh2r, px.at[0, 1], px.at[1, 1], core)
    gcp_x = rdma(gcp, gcr, px.at[0, 2], px.at[1, 2], core)
    m_x = rdma(h1, mr, px.at[0, 11], px.at[1, 11], core)
    load_w(0).wait()

    def chunk(k):
        slot = k % 2
        w = wbuf.at[slot]
        experts_tile(ROWS, w, h2, gm, cx, gca, m, gh2, cag)

        @pl.when(k < 7)
        def _():
            nxt = k + 1
            dz, dy = order(nxt)

            @pl.when(dz == 0)
            def _():
                w_y_in(dy).wait_recv()
                for way in (0, 1):
                    w_z(way, dy, zl).start()

            @pl.when(dz == 1)
            def _():
                for way in (0, 1):
                    w_z(way, dy, 1 - zl).wait_recv()

            load_w(nxt).start()

        @pl.when(k == 7)
        def _():
            cx[ROWS:] = gh2[ROWS:].astype(BF16)
            gh2_x.start()
            gcp[...] = dot_nt(gca[ROWS:].astype(BF16), expander())
            gcp_x.start()
            h1[...] = m[ROWS:].astype(BF16)
            m_x.start()

        experts_tile(0, w, h2, gm, cx, gca, m, gh2, cag)

        @pl.when(k >= 2)
        def _():
            sends(k - 2, 1)

        for b in range(2):
            gv = dot((h2t if b == 0 else gmt)[...], cag[:, (CH if b == 0 else 0) : (2 * CH if b == 0 else CH)])
            gst[slot, b] = gv.astype(BF16).reshape(4, 128, CH)
        sends(k, 0)

        @pl.when(k < 7)
        def _():
            load_w(k + 1).wait()

    loop(0, 8, chunk)

    glb, gab = comb.at[peer_rows], gm.at[peer_rows]
    p1a = wbuf.at[0].reshape(2, 4, 2, RA, CH)
    p1b = wbuf.at[1, :CH].reshape(2, 2, 4, RB, CH)
    p1c = wbuf.at[1, CH:].reshape(4, 4, RC, CH)
    gs = gst.reshape(4, 8, 64, D)
    p2a = ob.at[0:256].reshape(2, 2, RA, CH)
    p2b = ob.at[256:384].reshape(4, RB, CH)
    p2c = ob.at[384:512].reshape(4, RC, CH)
    fp = ob.at[512:640]

    gh2_x.wait_recv()
    gcp_x.wait_recv()
    m_x.wait_recv()

    def second(i):
        layer_result(i, tok, aux, x1, m, mr, out)
        second_norm_back(i, s_ref, mt, aux, gates, gca, gcr, gh2, gh2r, gm, x1, glb, gab, vec)

    loop(0, IMG, second)
    cag[ROWS:, D:] = dot_nt(gab[...], s_ref[:, 1536:2048]).astype(BF16)
    loop(0, 2, lambda i: attend_back(i, qkv, pb, cag))

    started = []

    def go(copies):
        for cp in copies:
            cp.start()
        started.extend(copies)
        return copies

    def arrived(copies):
        for cp in copies:
            cp.wait_recv()

    def by_x(src, dst, n):
        return [
            rdma(src(up(x, d)), dst(d), gsem.at[0, n, d], gsem.at[1, n, d], dev(x_=up(x, d))) for d in (1, 2, 3)
        ]

    def by_y(src, dst, n):
        return [
            rdma(src(up(y, d)), dst(d), gsem.at[0, n, d], gsem.at[1, n, d], dev(y_=up(y, d))) for d in (1, 2, 3)
        ]

    def by_z(src, dst, n):
        copies = []
        for q in (1, 2, 3):
            zhv, zlv = (zh + q // 2) % 2, (zl + q % 2) % 2
            copies.append(rdma(src(zlv, zhv), dst(q), gsem.at[0, n, q], gsem.at[1, n, q], dev(zh_=zhv, zl_=zlv)))
        return copies

    def total(first, rest):
        acc = first.astype(F32)
        for d in (1, 2, 3):
            acc = acc + rest[d].astype(F32)
        return acc.astype(BF16)

    sends(6, 1)
    sends(7, 1)
    la = gst.reshape(2, 4, 2, 2, RA, CH)
    lb = gst.reshape(2, 4, 2, 4, RB, CH)

    def first_sum(part, count, recv, src, buf, put):
        for d in (1, 2, 3):
            rdma(recv.at[d], recv.at[d], ssem.at[0, 0], rsem.at[part, d], core).wait_recv()

        def loads(n):
            return [pltpu.make_async_copy(src(s, n), buf.at[n % 2, s], asem.at[n % 2, s]) for s in range(4)]

        for cp in loads(0):
            cp.start()

        def one(n):
            @pl.when(n + 1 < count)
            def _():
                for cp in loads(n + 1):
                    cp.start()

            for cp in loads(n):
                cp.wait()
            v = buf.at[n % 2]
            put(n, total(v[0], v))

        loop(0, count, one)

    def put_a(n, v):
        p1a[n // 2, span(2 * (n % 2), 2, 2)] = v

    def put_b(n, v):
        p1b[n] = v

    def put_c(n, v):
        p1c[span(2 * n, 2, 2)] = v

    first_sum(0, 4, r1a, lambda s, n: r1a.at[s, n // 2, span(2 * (n % 2), 2, 2)], la, put_a)
    s2a = go(by_y(lambda v: p1a.at[:, v], lambda d: r2a.at[d], 0))
    first_sum(1, 2, r1b, lambda s, n: r1b.at[s, n], lb, put_b)
    s2b = go(by_z(lambda zlv, zhv: p1b.at[zlv, zhv], lambda d: r2b.at[d], 1))
    first_sum(2, 2, r1c, lambda s, n: r1c.at[s, span(2 * n, 2, 2)], lb, put_c)
    s2c = go(by_x(lambda v: p1c.at[:, v], lambda d: r2c.at[d], 2))

    loop(2, 4, lambda i: attend_back(i, qkv, pb, cag))

    for b in range(3):
        gv = dot(h1t[...], cag[:ROWS, D * b : D * b + D] if b < 2 else cag[ROWS:, :D])
        gs[b] = gv.astype(BF16).reshape(8, 64, D)
    gs[3] = dot_tn(ob[...], gab[...]).astype(BF16).reshape(8, 64, D)
    s_core = go([rdma(gs.at[:, :, span(32 * (1 - c), 32, 32)], cr, gsem.at[0, 3, 1], gsem.at[1, 3, 1], core)])

    arrived(s2a)
    p2a[...] = total(p1a[:, y], r2a)
    s3a = go(by_z(lambda zlv, zhv: p2a.at[zlv, zhv], lambda d: r3a.at[d], 4))
    arrived(s2b)
    p2b[...] = total(p1b[zl, zh], r2b)
    s3b = go(by_x(lambda v: p2b.at[v], lambda d: r3b.at[d], 5))
    arrived(s2c)
    p2c[...] = total(p1c[:, x], r2c)
    s3c = go(by_y(lambda v: p2c.at[v], lambda d: r3c.at[d], 6))

    last = lambda i: first_norm_back(i, tok, cot, aux, s_ref, mt, cag, x1, vec, gt)
    loop(0, 1, last)

    arrived(s_core)

    def core_sum(j):
        mine = gs[:, j, span(32 * c, 32, 32)]
        gc[:, j // 4, j % 4] = (mine.astype(F32) + cr[:, j].astype(F32)).astype(BF16)

    loop(0, 8, core_sum)
    t1a = go(by_x(lambda v: gc.at[v, :, :, 0:16], lambda d: qa1.at[d], 7))
    t1b = go(by_z(lambda zlv, zhv: gc.at[span(2 * zhv, 2, 2), zlv, :, 16:32], lambda d: qb1.at[d], 8))

    loop(1, IMG, last)

    arrived(s3a)
    fp[:RA] = total(p2a[zl, zh], r3a)
    arrived(s3b)
    fp[RA : RA + RB] = total(p2b[x], r3b)
    arrived(s3c)
    fp[RA + RB :] = total(p2c[y], r3c)
    f_own = pltpu.make_async_copy(fp, f_all.at[c, zh, x], lsem.at[0])
    f_own.start()
    f_z = go([rdma(fp, f_all.at[c, zh, x], gsem.at[0, 9, 1], gsem.at[1, 9, 1], dev(zh_=1 - zh))])

    mr_g = dot_tn(glb[...], h2[:ROWS])
    row = lax.broadcasted_iota(jnp.int32, (8, D), 0)
    mx[0, c] = jnp.where(row < 4, mr_g[:8], vec[...])

    def misc_go(n, me, targets):
        return go([rdma(mx.at[n, me], mx.at[n, me], msem.at[0, n, d], msem.at[1, n, d], t) for d, t in targets])

    def misc_sum(n, count):
        acc = mx[n, 0]
        for i in range(1, count):
            acc = acc + mx[n, i]
        return acc

    m0 = misc_go(0, c, [(1, core)])

    arrived(t1a)
    ga2[...] = total(gc[x, :, :, 0:16], qa1)
    t2a = go(by_y(lambda v: ga2.at[:, v], lambda d: qa2.at[d], 10))
    arrived(t1b)
    gb2[...] = total(gc[span(2 * zh, 2, 2), zl, :, 16:32], qb1)
    t2b = go(by_x(lambda v: gb2.at[v // 2, :, :, span(256 * (v % 2), 256, 256)], lambda d: qb2.at[d], 11))

    arrived(m0)
    mx[1, x] = misc_sum(0, 2)
    m1 = misc_go(1, x, [(d, dev(x_=up(x, d))) for d in (1, 2, 3)])

    f_own.wait()
    arrived(f_z)
    f_x = go(by_x(lambda v: f_all.at[c, :, x], lambda d: f_all.at[c, :, x], 12))

    arrived(t2a)
    ga3[...] = total(ga2[:, y], qa2)
    t3a = go(by_z(lambda zlv, zhv: ga3.at[zlv, :, span(256 * zhv, 256, 256)], lambda d: qa3.at[d], 13))
    arrived(t2b)
    gb3[...] = total(gb2[x // 2, :, :, span(256 * (x % 2), 256, 256)], qb2)
    t3b = go(by_y(lambda v: gb3.at[v], lambda d: qb3.at[d], 14))

    arrived(m1)
    mx[2, y] = misc_sum(1, 4)
    m2 = misc_go(2, y, [(d, dev(y_=up(y, d))) for d in (1, 2, 3)])

    arrived(f_x)
    f_c = go([rdma(f_all.at[c], f_all.at[c], gsem.at[0, 15, 1], gsem.at[1, 15, 1], core)])

    arrived(t3a)
    la_own = span(512 * x + 256 * zh, 256, 256)
    sf[c, 0:16, la_own] = total(ga3[zl, :, span(256 * zh, 256, 256)], qa3)
    arrived(t3b)
    lb_own = span(1024 * zh + 256 * x, 256, 256)
    sf[c, 16:32, lb_own] = total(gb3[y], qb3)
    across = dev(zh_=1 - zh)
    wa, wb = sf.at[c, 0:16, la_own], sf.at[c, 16:32, lb_own]
    t4 = go(
        [
            rdma(wa, wa, gsem.at[0, 16, 1], gsem.at[1, 16, 1], across),
            rdma(wb, wb, gsem.at[0, 16, 2], gsem.at[1, 16, 2], across),
        ]
    )

    arrived(m2)
    mx[3, z] = misc_sum(2, 4)
    m3 = misc_go(3, z, [(d, dev_z(up(z, d))) for d in (1, 2, 3)])

    arrived(t4)
    wins = [
        sf.at[c, 0:16, span(512 * x, 512, 512)],
        sf.at[c, 16:32, span(256 * x, 256, 256)],
        sf.at[c, 16:32, span(1024 + 256 * x, 256, 256)],
    ]
    t5 = []
    for i, w in enumerate(wins):
        t5 += by_x(lambda v, w=w: w, lambda d, w=w: w, 17 + i)
    go(t5)
    arrived(m3)
    misc[...] = misc_sum(3, 4)
    arrived(t5)
    t6 = go([rdma(sf.at[c], sf.at[c], gsem.at[0, 20, 1], gsem.at[1, 20, 1], core)])
    arrived(f_c)
    arrived(t6)

    for cp in started:
        cp.wait_send()
    for cp in [gm_x, gh2_x, gcp_x, m_x]:
        cp.wait_send()
    loop(0, IMG, lambda i: (h2_x(i).wait_send(), comb_x(i).wait_send()))
    for d in (1, 2, 3):
        s_y(d).wait_send()
        w_y(d).wait_send()
    for d in range(4):
        for way in (0, 1):
            s_z(way, d).wait_send()
            w_z(way, d, zl).wait_send()
        for dz in (0, 1):
            if (dz, d) != (0, 0):
                s_c(dz, d).wait_send()


def per_device(
    tokens, key_mask, image_live, routes, ln1_gain, ln1_bias, w_qkv, w_attn, ln2_gain, ln2_bias,
    w_router, w_in, w_out, cotangent,
):
    images, length, width = tokens.shape
    vecs = jnp.stack([ln1_gain, ln1_bias, ln2_gain, ln2_bias], axis=1)
    pack = jnp.concatenate([w_qkv, w_attn, w_router, vecs, jnp.zeros((64, 120), BF16)], axis=1)
    kb = jnp.where(key_mask > 0, 0.0, NEG).astype(F32)
    kb = jnp.pad(kb, ((0, 0), (0, PAD - LEN)), constant_values=NEG)[:, None, :]
    ids = jnp.arange(128, dtype=jnp.int32)[None, None, :]
    flags = (routes[:, :, 0:1] == ids) | (routes[:, :, 1:2] == ids) | ((image_live[:, None, None] > 0) & (ids == 4))
    aux = jnp.pad(flags.astype(BF16), ((0, 0), (0, PAD - LEN), (0, 0))).reshape(ROWS, 128)

    sds = jax.ShapeDtypeStruct
    vm = pl.BlockSpec(memory_space=pltpu.VMEM)
    hbm = pl.BlockSpec(memory_space=pl.ANY)
    V = pltpu.VMEM
    S = pltpu.SemaphoreType.DMA
    outs = pl.pallas_call(
        kernel,
        in_specs=[vm, vm, vm, vm, hbm, hbm, hbm],
        out_specs=[vm, vm, vm, vm, hbm, hbm, hbm, hbm, hbm],
        out_shape=[
            sds((IMG, LEN, D), BF16),
            sds((IMG, LEN, D), F32),
            sds((2, 32, 2048), BF16),
            sds((8, D), F32),
            sds((8, 2 * CH, D), BF16),
            sds((2, 2, 4, 128, CH), BF16),
            sds((4, 2, 4, 2, RA, CH), BF16),
            sds((4, 2, 2, 4, RB, CH), BF16),
            sds((4, 4, 4, RC, CH), BF16),
        ],
        scratch_shapes=[
            V((D, 2176), BF16),
            V((2, 2 * CH, D), BF16),
            V((2, 2, 4, 128, CH), BF16),
            V((ROWS, D), BF16),
            V((D, ROWS), BF16),
            V((ROWS, 3 * D), BF16),
            V((IMG * HEADS, PAD, PAD), BF16),
            V((ROWS, D), BF16),
            V((ROWS, D), F32),
            V((PAIR, D), BF16),
            V((PAIR, D), BF16),
            V((D, PAIR), BF16),
            V((D, PAIR), BF16),
            V((ROWS, 128), F32),
            V((PAIR, 128), BF16),
            V((PAIR, CH), BF16),
            V((PAIR, D), F32),
            V((PAIR, D), F32),
            V((PAIR, CH), F32),
            V((PAIR, 2 * CH), BF16),
            V((ROWS, D), BF16),
            V((ROWS, D), BF16),
            V((ROWS, 128), F32),
            V((ROWS, 128), F32),
            V((8, D), F32),
            V((8, D), F32),
            V((4, 4, 8, D), F32),
            V((4, 8, 32, 512), BF16),
            V((4, 2, 4, 32, 512), BF16),
            V((4, 2, 4, 16, 512), BF16),
            V((4, 2, 4, 16, 512), BF16),
            V((4, 2, 16, 512), BF16),
            V((4, 4, 16, 256), BF16),
            V((4, 16, 256), BF16),
            V((4, 16, 256), BF16),
            V((2, 4, 16, 512), BF16),
            V((2, 4, 16, 512), BF16),
            V((2, 16, 512), BF16),
            V((4, 16, 256), BF16),
            V((4, 2, 2, RA, CH), BF16),
            V((4, 4, RB, CH), BF16),
            V((4, 4, RC, CH), BF16),
            V((4, RA, CH), BF16),
            V((4, RB, CH), BF16),
            V((4, RC, CH), BF16),
            S((9,)),
            S((2, 4)),
            S((2, 2, 4)),
            S((2, 2, 4)),
            S((2, 4)),
            S((2, 2, 4)),
            S((2, 12)),
            S((2, 6)),
            S((2, 3)),
            S((3, 4)),
            S((2, 4)),
            S((2, 21, 4)),
            S((2, 4, 4)),
            S((2,)),
        ],
        compiler_params=pltpu.CompilerParams(
            collective_id=0, has_side_effects=True, vmem_limit_bytes=61 * 1024 * 1024
        ),
        cost_estimate=pl.CostEstimate(flops=50_000_000_000, bytes_accessed=60_000_000, transcendentals=10_000_000),
        name="layer",
    )(tokens, kb, aux, cotangent, pack, w_in, w_out)
    layer_out, grad_tokens, sf, misc, _, f_all = outs[:6]
    small = sf.reshape(64, 2048).astype(F32)
    mine = lax.dynamic_slice(misc, (0, 64 * lax.axis_index("fsdp")), (8, 64))
    f = f_all.reshape(2, 2, D, 4, 128).astype(F32)
    g_in = f[:, 0].transpose(2, 1, 0, 3).reshape(4, D, 256)
    g_out = f[:, 1].transpose(2, 0, 3, 1).reshape(4, 256, D)
    return (
        layer_out, grad_tokens, mine[4], mine[5], small[:, :1536], small[:, 1536:], mine[6], mine[7],
        mine[:4].T, g_in, g_out,
    )


def solution(mesh):
    dev = ("dp", "fsdp", "seq")
    in_specs = (
        P(dev, None, None), P(dev, None), P(dev), P(dev, None, None), P("fsdp"), P("fsdp"), P("fsdp", None),
        P("fsdp", None), P("fsdp"), P("fsdp"), P("fsdp", None), P(None, None, "fsdp"), P(None, "fsdp", None),
        P(dev, None, None),
    )
    out_specs = (
        P(dev, None, None), P(dev, None, None), P("fsdp"), P("fsdp"), P("fsdp", None), P("fsdp", None), P("fsdp"),
        P("fsdp"), P("fsdp", None), P(None, None, "fsdp"), P(None, "fsdp", None),
    )
    return jax.shard_map(per_device, mesh=mesh, in_specs=in_specs, out_specs=out_specs, check_vma=False)
```

```python
import jax
import jax.numpy as jnp
from jax import lax
from jax.experimental import pallas as pl
from jax.experimental.pallas import tpu as pltpu
from jax.sharding import PartitionSpec as P

F32 = jnp.float32
BF16 = jnp.bfloat16
MESH = pl.DeviceIdType.MESH
HEADS = 8
EPS = 1e-06
NEG = -1000000000.0
D = 512
IMG = 4
LEN = 200
PAD = 208
ROWS = IMG * PAD
PAIR = 2 * ROWS
HD = 64
CH = 512
TM = 832
RA, RB, RC = 48, 48, 32


def dot(a, b):
    return jnp.dot(a, b, preferred_element_type=F32)


def dot_nt(a, b):
    return lax.dot_general(a, b, (((1,), (1,)), ((), ())), preferred_element_type=F32)


def dot_tn(a, b):
    return lax.dot_general(a, b, (((0,), (0,)), ((), ())), preferred_element_type=F32)


def rows_of(i):
    return pl.ds(pl.multiple_of(i * PAD, 16), PAD)


def span(start, size, unit):
    return pl.ds(pl.multiple_of(start, unit), size)


def pad_rows(v):
    return jnp.concatenate([v, jnp.zeros((PAD - LEN, v.shape[1]), v.dtype)], axis=0)


def normalize(v):
    c = v - jnp.mean(v, axis=-1, keepdims=True)
    r = lax.rsqrt(jnp.mean(c * c, axis=-1, keepdims=True) + EPS)
    return c * r, r


def lane(shape):
    return lax.broadcasted_iota(jnp.int32, shape, 1)


def loop(lo, hi, body):
    def step(i, carry):
        body(i)
        return carry

    lax.fori_loop(lo, hi, step, 0)


def norm_back(u, n, r):
    return r * (u - jnp.mean(u, axis=-1, keepdims=True) - n * jnp.mean(u * n, axis=-1, keepdims=True))


def ln_one(tok, mt, h1):
    def body(i):
        n, _ = normalize(pad_rows(tok[i].astype(F32)))
        h1[rows_of(i)] = (n * mt[4:5] + mt[5:6]).astype(BF16)

    loop(0, IMG, body)


def make_qkv(s_ref, h1, qkv):
    for b in range(3):
        v = dot(h1[...], s_ref[:, D * b : D * b + D]).astype(BF16)
        if b == 0:
            v = v * jnp.asarray(HD**-0.5, BF16)
        qkv[:, D * b : D * b + D] = v


def attend(i, qkv, prep, pb, ob):
    r = rows_of(i)
    bias = prep[i, 2:3, :PAD]
    low = lane((PAD, 128)) < HD
    for hp in range(HEADS // 2):
        o = 128 * hp
        q2, k2, v2 = qkv[r, o : o + 128], qkv[r, D + o : D + o + 128], qkv[r, 2 * D + o : 2 * D + o + 128]
        outs = []
        for a in range(2):
            qm = jnp.where(low if a == 0 else ~low, q2, jnp.zeros_like(q2))
            s = dot_nt(qm, k2) + bias
            e = jnp.exp(s - jnp.max(s, axis=-1, keepdims=True))
            p = (e * (1.0 / jnp.sum(e, axis=-1, keepdims=True))).astype(BF16)
            pb[i * HEADS + hp * 2 + a] = p
            outs.append(dot(p, v2))
        ob[r, o : o + 128] = jnp.where(low, outs[0], outs[1]).astype(BF16)


def middle(i, tok, s_ref, mt, mtb, ob, aux, x1, h2, gates, comb):
    r = rows_of(i)
    v = pad_rows(tok[i].astype(F32)) + dot(ob[r], s_ref[:, 3 * D :])
    x1[r] = v
    n, _ = normalize(v)
    h = (n * mt[6:7] + mt[7:8]).astype(BF16)
    h2[r] = h
    lg = dot_nt(h, mtb[...])
    ok = lane((PAD, 128)) < 4
    lg = jnp.where(ok, lg, -1e30)
    e = jnp.exp(lg - jnp.max(lg, axis=-1, keepdims=True))
    g = e / jnp.sum(e, axis=-1, keepdims=True)
    gates[r] = g
    comb[r] = jnp.where(ok, g * aux[r].astype(F32), 0.0).astype(BF16)


def masks(i, prep, aux):
    row = lax.broadcasted_iota(jnp.int32, (128, 256), 0)
    v = prep[i]
    e = row.astype(F32)
    hit = ((v[0:1] == e) | (v[1:2] == e)) & (row < 4)
    flags = jnp.where(hit, 1.0, jnp.where(row == 4, v[3:4], 0.0))
    aux[rows_of(i)] = jnp.transpose(flags)[:PAD].astype(BF16)


def live_cotangent(i, cot, aux, gm):
    r = rows_of(i)
    gm[r] = (pad_rows(cot[i].astype(F32)) * aux[r, 4:5].astype(F32)).astype(BF16)


def expander():
    return (
        lax.broadcasted_iota(jnp.int32, (128, CH), 0) == lax.broadcasted_iota(jnp.int32, (128, CH), 1) // 128
    ).astype(BF16)


def experts_tile(lo, w, h2, gm, cx, gca, m, gh2, cag):
    r = pl.ds(lo, TM)
    win, wout = w[:CH], w[CH:]
    hid = dot(h2[r], win)
    ga = dot_nt(gm[r], wout)
    cdf = 0.5 * (1.0 + lax.erf(hid * 0.7071067811865476))
    slope = cdf + hid * jnp.exp(-0.5 * hid * hid) * 0.3989422804014327
    act = hid * cdf
    c = cx[r].astype(F32)
    gca[r] += act * ga
    ca = (act * c).astype(BF16)
    gh = (ga * c * slope).astype(BF16)
    cag[r, :CH] = ca
    cag[r, CH:] = gh
    m[r] += dot(ca, wout)
    gh2[r] += dot_nt(gh, win)


def layer_result(i, tok, aux, m, mr, out):
    r = rows_of(i)
    v = m[r] + mr[r].astype(F32)
    out[i] = jnp.where(aux[r, 4:5].astype(F32) > 0, v, pad_rows(tok[i].astype(F32)))[:LEN].astype(BF16)


def second_norm_back(i, mtb, mt, aux, gates, gca, gcr, gh2, gh2r, gm, x1, m, glb, gab, vec):
    r = rows_of(i)
    ok = lane((PAD, 128)) < 4
    ch = jnp.where(ok, aux[r].astype(F32), 0.0)
    g = gates[r]
    gg = (dot_nt(gca[r].astype(BF16), expander()) + gcr[r]) * ch
    gl = (g * (gg - jnp.sum(gg * g, axis=-1, keepdims=True))).astype(BF16)
    glb[r] = gl
    gh = gh2[r] + gh2r[r].astype(F32) + dot(gl, mtb[...])
    n, r2 = normalize(x1[r])
    vec[6:7] += jnp.sum(gh * n, axis=0, keepdims=True)
    vec[7:8] += jnp.sum(gh, axis=0, keepdims=True)
    gx = gm[r].astype(F32) + norm_back(gh * mt[6:7], n, r2)
    m[r] += x1[r]
    x1[r] = gx
    gab[r] = gx.astype(BF16)


def attend_back(i, qkv, pb, cag):
    r = rows_of(i)
    rv = span(ROWS + i * PAD, PAD, 16)
    low = lane((PAD, 128)) < HD
    for hp in range(HEADS // 2):
        o = 128 * hp
        q2, k2, v2 = qkv[r, o : o + 128], qkv[r, D + o : D + o + 128], qkv[r, 2 * D + o : 2 * D + o + 128]
        g2 = cag[rv, D + o : D + o + 128]
        gq, gk, gv = [], [], []
        for a in range(2):
            gmk = jnp.where(low if a == 0 else ~low, g2, jnp.zeros_like(g2))
            p = pb[i * HEADS + hp * 2 + a]
            pf = p.astype(F32)
            t = dot_nt(gmk, v2)
            gs = (pf * (t - jnp.sum(t * pf, axis=-1, keepdims=True))).astype(BF16)
            gq.append(dot(gs, k2))
            gk.append(dot_tn(gs, q2))
            gv.append(dot_tn(p, g2))
        cag[r, o : o + 128] = (jnp.where(low, gq[0], gq[1]) * HD**-0.5).astype(BF16)
        cag[r, D + o : D + o + 128] = jnp.where(low, gk[0], gk[1]).astype(BF16)
        cag[rv, o : o + 128] = jnp.where(low, gv[0], gv[1]).astype(BF16)


def first_norm_back(i, tok, cot, aux, s_ref, mt, cag, x1, vec, gt):
    r = rows_of(i)
    rv = span(ROWS + i * PAD, PAD, 16)
    gh = (
        dot_nt(cag[r, :D], s_ref[:, :D])
        + dot_nt(cag[r, D:], s_ref[:, D : 2 * D])
        + dot_nt(cag[rv, :D], s_ref[:, 2 * D : 3 * D])
    )
    n, r1 = normalize(pad_rows(tok[i].astype(F32)))
    vec[4:5] += jnp.sum(gh * n, axis=0, keepdims=True)
    vec[5:6] += jnp.sum(gh, axis=0, keepdims=True)
    gd = jnp.where(aux[r, 4:5].astype(F32) > 0, 0.0, pad_rows(cot[i].astype(F32)))
    gt[i] = (gd + x1[r] + norm_back(gh * mt[4:5], n, r1))[:LEN]


def order(k):
    dy = jnp.where((k == 1) | (k == 4), 2, jnp.where((k == 2) | (k == 5), 1, jnp.where((k == 3) | (k == 6), 3, 0)))
    dz = jnp.where(k >= 4, 1, 0)
    return dz, dy


def kernel(
    tok, prep, cot, q_in, a_in, v_in, w_in, w_out,
    out, gt, sf, misc, w_all, f_all, r1a, r1b, r1c,
    s_ref, wbuf, gst, h1, h1t, qkv, pb, ob, x1, h2, gm, h2t, gmt, gates, comb, cx, m, gh2, gca, cag,
    gh2r, mr, gcp, gcr, mt, vec, mx, aux, mtg, mtb,
    cr, gc, qa1, qb1, qa2, qb2, qa3, qb3, ga2, gb2, ga3, gb3, r2a, r2b, r2c,
    r3a, r3b, r3c,
    lsem, sy, sz, sc, vy, vz, wy, wx, wz, px, ssem, lsem2, rsem, asem, gsem, msem, wsem, bsem,
):
    zh, f, sq = lax.axis_index("dp"), lax.axis_index("fsdp"), lax.axis_index("seq")
    zl, y = f // 4, f % 4
    x, c = sq // 2, sq % 2
    z = zh * 2 + zl

    def dev(zh_=zh, zl_=zl, y_=y, x_=x, c_=c):
        return (zh_, zl_ * 4 + y_, x_ * 2 + c_)

    def up(v, d):
        return (v + d) % 4

    def dev_z(zz):
        return dev(zh_=zz // 2, zl_=zz % 2)

    core = dev(c_=1 - c)

    def rdma(src, dst, ssm, rsm, target):
        return pltpu.make_async_remote_copy(
            src_ref=src, dst_ref=dst, send_sem=ssm, recv_sem=rsm, device_id=target, device_id_type=MESH
        )

    barrier = pltpu.get_barrier_semaphore()
    for d in (1, 2, 3):
        for target in (dev(x_=up(x, d)), dev(y_=up(y, d)), dev_z(up(z, d))):
            pl.semaphore_signal(barrier, inc=1, device_id=target, device_id_type=MESH)
    others = [(1, 0, 0)] + [(dc, dzh, d) for dc in (0, 1) for dzh in (0, 1) for d in range(4) if d and dc + dzh]
    others += [(1, 1, 0)]
    for dc, dzh, d in others:
        target = dev(c_=(c + dc) % 2, zh_=(zh + dzh) % 2, x_=up(x, d))
        pl.semaphore_signal(barrier, inc=1, device_id=target, device_id_type=MESH)

    own = [
        pltpu.make_async_copy(q_in, s_ref.at[span(64 * f, 64, 64), : 3 * D], lsem.at[0]),
        pltpu.make_async_copy(a_in, s_ref.at[span(64 * f, 64, 64), 3 * D :], lsem.at[9]),
        pltpu.make_async_copy(v_in, mtg.at[f], lsem.at[10]),
    ]
    half = span(128 * c, 128, 128)
    for e in range(4):
        own.append(
            pltpu.make_async_copy(w_in.at[e, :, half], wbuf.at[0, :CH, 128 * e : 128 * e + 128], lsem.at[1 + e])
        )
        own.append(
            pltpu.make_async_copy(w_out.at[e, half, :], wbuf.at[0, CH + 128 * e : CH + 128 * e + 128], lsem.at[5 + e])
        )
    for cp in own:
        cp.start()
    pl.semaphore_wait(barrier, 9 + len(others))
    for cp in own[:3]:
        cp.wait()

    cols = (slice(0, 3 * D), slice(3 * D, 4 * D))

    def s_part(p, zz, yy, cc, size=32, off=0):
        return s_ref.at[span((zz * 4 + yy) * 64 + 32 * cc + off, size, 16), cols[p]]

    def s_y(p, d):
        r = s_part(p, zl, y, c)
        return rdma(r, r, sy.at[0, p, d], sy.at[1, p, d], dev(y_=up(y, d)))

    def s_z(p, way, d):
        r = s_part(p, zl, up(y, 4 - d), c, 16, 16 * way)
        return rdma(r, r, sz.at[0, p, way, d], sz.at[1, p, way, d], dev_z(up(z, 1 if way == 0 else 3)))

    def s_c(p, dz, d):
        r = s_part(p, (zl + dz) % 2, up(y, 4 - d), c)
        return rdma(r, r, sc.at[0, p, dz, d], sc.at[1, p, dz, d], core)

    def v_y(d):
        return rdma(mtg.at[f], mtg.at[f], vy.at[0, d], vy.at[1, d], dev(y_=up(y, d)))

    def v_z(d):
        r = mtg.at[zl * 4 + up(y, 4 - d)]
        return rdma(r, r, vz.at[0, d], vz.at[1, d], dev_z(up(z, 1)))

    def s_z_done(p):
        for d in (0, 1, 3, 2):
            for way in (0, 1):
                s_z(p, way, d).wait_recv()
            s_c(p, 1, d).start()

    def s_c_done(p):
        for dz in (0, 1):
            for d in range(4):
                if (dz, d) != (0, 0):
                    s_c(p, dz, d).wait_recv()

    for d in (1, 3, 2):
        v_y(d).start()
    v_z(0).start()
    for p in (0, 1):
        for d in (1, 3, 2):
            s_y(p, d).start()
        for way in (0, 1):
            s_z(p, way, 0).start()

    loop(0, IMG, lambda i: (masks(i, prep, aux), live_cotangent(i, cot, aux, gm)))
    own_rows, peer_rows = pl.ds(0, ROWS), pl.ds(ROWS, ROWS)
    gm_x = rdma(gm.at[own_rows], gm.at[peer_rows], px.at[0, 0], px.at[1, 0], core)

    for d in (1, 3, 2):
        v_y(d).wait_recv()
        v_z(d).start()
    for p in (0, 1):
        for d in (1, 3, 2):
            s_y(p, d).wait_recv()
            for way in (0, 1):
                s_z(p, way, d).start()
            s_c(p, 0, d).start()

    def w_y(d, h=0):
        r = w_all.at[f, span(256 * x, 256, 256)] if d == 2 else w_all.at[f, CH * h : CH * h + CH]
        return rdma(r, r, wy.at[0, d + 4 * h], wy.at[1, d + 4 * h], dev(y_=up(y, d)))

    def w_x(n, d):
        dz, dy = ((0, 2), (1, 0), (1, 2))[n]
        r = w_all.at[((zl + dz) % 2) * 4 + up(y, dy), span(256 * x, 256, 256)]
        return rdma(r, r, wx.at[0, n, d], wx.at[1, n, d], dev(x_=up(x, d)))

    def w_z(way, d, h=0):
        chunk_of = w_all.at[zl * 4 + up(y, 4 - d)]
        if d % 2 == 0:
            r = chunk_of.at[span(256 * x + 128 * way, 128, 128)]
        else:
            r = chunk_of.at[CH * h + 256 * way : CH * h + 256 * way + 256]
        return rdma(r, r, wz.at[0, way, d + 4 * h], wz.at[1, way, d + 4 * h], dev_z(up(z, 1 if way == 0 else 3)))

    all_w_y = [(2, 0), (1, 0), (3, 0), (1, 1), (3, 1)]
    all_w_z = [(way, d, h) for d, h in [(0, 0), (2, 0), (1, 0), (3, 0), (1, 1), (3, 1)] for way in (0, 1)]

    for cp in own[3:]:
        cp.wait()
    w_own = pltpu.make_async_copy(wbuf.at[0], w_all.at[f], lsem.at[0])
    w_own.start()
    w_own.wait()
    for d, h in all_w_y:
        w_y(d, h).start()

    gm_x.start()
    gmt[:, :ROWS] = gm[:ROWS].T
    for d in range(4):
        v_z(d).wait_recv()
    mt[...] = jnp.concatenate([(mtg[2 * i, :8] + mtg[2 * i + 1, :8]).astype(F32) for i in range(4)], axis=1)
    mtb[...] = jnp.concatenate([mt[...], jnp.zeros((120, D), F32)], axis=0).astype(BF16)
    vec[...] = jnp.zeros_like(vec)
    s_z_done(0)
    for way in (0, 1):
        w_z(way, 0).start()
    ln_one(tok, mt, h1)
    s_c_done(0)

    make_qkv(s_ref, h1, qkv)
    s_z_done(1)
    w_y(2).wait_recv()
    for d in (1, 2, 3):
        w_x(0, d).start()
    for way in (0, 1):
        w_z(way, 2).start()
    for way in (0, 1):
        w_z(way, 0).wait_recv()
    for d in (1, 2, 3):
        w_x(1, d).start()
    s_c_done(1)

    def h2_x(i):
        return rdma(h2.at[rows_of(i)], h2.at[span(ROWS + i * PAD, PAD, 16)], px.at[0, 3 + i], px.at[1, 3 + i], core)

    def comb_x(i):
        return rdma(comb.at[rows_of(i)], comb.at[span(ROWS + i * PAD, PAD, 16)], px.at[0, 7 + i], px.at[1, 7 + i], core)

    def forward(i):
        attend(i, qkv, prep, pb, ob)
        middle(i, tok, s_ref, mt, mtb, ob, aux, x1, h2, gates, comb)
        h2_x(i).start()
        comb_x(i).start()

    loop(0, 2, forward)
    for d in (1, 3):
        w_y(d, 0).wait_recv()
        for way in (0, 1):
            w_z(way, d, 0).start()
    loop(2, IMG, forward)
    for way in (0, 1):
        w_z(way, 2).wait_recv()
    for d in (1, 2, 3):
        w_x(2, d).start()
    gm_x.wait_recv()
    gmt[:, ROWS:] = gm[ROWS:].T
    h1t[...] = h1[...].T
    h2t[:, :ROWS] = h2[:ROWS].T

    def load_w(k):
        dz, dy = order(k)
        return pltpu.make_async_copy(w_all.at[((zl + dz) % 2) * 4 + up(y, 4 - dy)], wbuf.at[k % 2], wsem.at[k % 2])

    m[...] = jnp.zeros_like(m)
    gh2[...] = jnp.zeros_like(gh2)
    gca[...] = jnp.zeros_like(gca)
    ex = expander()
    cx[:ROWS] = dot(comb[:ROWS], ex).astype(BF16)
    loop(0, IMG, lambda i: (h2_x(i).wait_recv(), comb_x(i).wait_recv()))
    h2t[:, ROWS:] = h2[ROWS:].T
    cx[ROWS:] = dot(comb[ROWS:], ex).astype(BF16)

    def sends(k, act):
        slot = k % 2
        dz, dy = order(k)
        zz, yy = (zl + dz) % 2, up(y, 4 - dy)

        def local(src, dst, i):
            cp = pltpu.make_async_copy(src, dst, lsem2.at[slot, i])
            cp.start() if act == 0 else cp.wait()

        def remote(src, dst, i, rsm, target):
            cp = rdma(src, dst, ssem.at[slot, i], rsm, target)
            cp.start() if act == 0 else cp.wait_send()

        g = gst.at[slot]
        for d in (1, 2, 3):
            remote(g.at[:, up(x, d), :RA], r1a.at[d, zz, yy], d - 1, rsem.at[0, d], dev(x_=up(x, d)))
        local(g.at[:, x, :RA], r1a.at[0, zz, yy], 0)

        @pl.when(dy != 0)
        def _():
            remote(g.at[:, :, RA : RA + RB], r1b.at[dy, zz], 3, rsem.at[1, dy], dev(y_=yy))

        @pl.when(dy == 0)
        def _():
            local(g.at[:, :, RA : RA + RB], r1b.at[0, zz], 1)

        remote(g.at[1 - zh, :, RA + RB :], r1c.at[2 + dz, yy], 4, rsem.at[2, 2 + dz], dev(zh_=1 - zh, zl_=zz))

        @pl.when(dz != 0)
        def _():
            remote(g.at[zh, :, RA + RB :], r1c.at[1, yy], 5, rsem.at[2, 1], dev(zl_=zz))

        @pl.when(dz == 0)
        def _():
            local(g.at[zh, :, RA + RB :], r1c.at[0, yy], 2)

    gh2_x = rdma(cx.at[peer_rows], gh2r, px.at[0, 1], px.at[1, 1], core)
    gcp_x = rdma(gcp, gcr, px.at[0, 2], px.at[1, 2], core)
    m_x = rdma(h1, mr, px.at[0, 11], px.at[1, 11], core)

    def chunk(k):
        slot = k % 2
        w = wbuf.at[slot]
        experts_tile(ROWS, w, h2, gm, cx, gca, m, gh2, cag)

        @pl.when(k < 7)
        def _():
            nxt = k + 1

            for n, part in ((1, 0), (4, 2), (7, 1)):

                @pl.when(nxt == n)
                def _(part=part):
                    for d in (1, 2, 3):
                        w_x(part, d).wait_recv()

            @pl.when(nxt == 2)
            def _():
                for d in (1, 3):
                    w_y(d, 1).wait_recv()
                    for way in (0, 1):
                        w_z(way, d, 1).start()

            for n, d in ((5, 1), (6, 3)):

                @pl.when(nxt == n)
                def _(d=d):
                    for h in (0, 1):
                        for way in (0, 1):
                            w_z(way, d, h).wait_recv()

            load_w(nxt).start()

        @pl.when(k == 7)
        def _():
            cx[ROWS:] = gh2[ROWS:].astype(BF16)
            gh2_x.start()
            gcp[...] = dot_nt(gca[ROWS:].astype(BF16), expander())
            gcp_x.start()
            h1[...] = m[ROWS:].astype(BF16)
            m_x.start()

        experts_tile(0, w, h2, gm, cx, gca, m, gh2, cag)

        @pl.when(k >= 2)
        def _():
            sends(k - 2, 1)

        for b in range(2):
            gv = dot((h2t if b == 0 else gmt)[...], cag[:, (CH if b == 0 else 0) : (2 * CH if b == 0 else CH)])
            gst[slot, b] = gv.astype(BF16).reshape(4, 128, CH)
        sends(k, 0)

        @pl.when(k < 7)
        def _():
            load_w(k + 1).wait()

    loop(0, 8, chunk)

    glb, gab = comb.at[peer_rows], gm.at[peer_rows]
    flat = wbuf.reshape(4 * CH, D)
    p1a = flat.at[: 16 * RA].reshape(2, 4, 2, RA, CH)
    p1b = flat.at[16 * RA : 16 * (RA + RB)].reshape(2, 2, 4, RB, CH)
    p1c = flat.at[16 * (RA + RB) :].reshape(4, 4, RC, CH)
    gs = gst.reshape(4, 8, 64, D)
    p2a = ob.at[: 4 * RA].reshape(2, 2, RA, CH)
    p2b = ob.at[4 * RA : 4 * (RA + RB)].reshape(4, RB, CH)
    p2c = ob.at[4 * (RA + RB) : 512].reshape(4, RC, CH)
    fp = ob.at[512:640]

    gh2_x.wait_recv()
    gcp_x.wait_recv()
    def second(i):
        second_norm_back(i, mtb, mt, aux, gates, gca, gcr, gh2, gh2r, gm, x1, m, glb, gab, vec)

    loop(0, IMG, second)
    cag[ROWS:, D:] = dot_nt(gab[...], s_ref[:, 3 * D :]).astype(BF16)
    loop(0, 1, lambda i: attend_back(i, qkv, pb, cag))

    started = []

    def go(copies):
        for cp in copies:
            cp.start()
        started.extend(copies)
        return copies

    def arrived(copies):
        for cp in copies:
            cp.wait_recv()

    def by_x(src, dst, n):
        return [
            rdma(src(up(x, d)), dst(d), gsem.at[0, n, d], gsem.at[1, n, d], dev(x_=up(x, d))) for d in (1, 2, 3)
        ]

    def by_y(src, dst, n):
        return [
            rdma(src(up(y, d)), dst(d), gsem.at[0, n, d], gsem.at[1, n, d], dev(y_=up(y, d))) for d in (1, 2, 3)
        ]

    def by_z(src, dst, n):
        copies = []
        for q in (1, 2, 3):
            zhv, zlv = (zh + q // 2) % 2, (zl + q % 2) % 2
            copies.append(rdma(src(zlv, zhv), dst(q), gsem.at[0, n, q], gsem.at[1, n, q], dev(zh_=zhv, zl_=zlv)))
        return copies

    def total(first, rest):
        acc = first.astype(F32)
        for d in (1, 2, 3):
            acc = acc + rest[d].astype(F32)
        return acc.astype(BF16)

    sends(6, 1)
    sends(7, 1)
    la = gst.reshape(2, 4, 2, 2, 64, CH)
    lb = gst.reshape(2, 4, 4, 64, CH)
    lc = gst.reshape(2, 4, 2, 4, RC, CH)

    def first_sum(part, count, recv, src, buf, put):
        for d in (1, 2, 3):
            rdma(recv.at[d], recv.at[d], ssem.at[0, 0], rsem.at[part, d], core).wait_recv()

        def loads(n):
            return [pltpu.make_async_copy(src(s, n), buf(n % 2).at[s], asem.at[n % 2, s]) for s in range(4)]

        for cp in loads(0):
            cp.start()

        def one(n):
            @pl.when(n + 1 < count)
            def _():
                for cp in loads(n + 1):
                    cp.start()

            for cp in loads(n):
                cp.wait()
            v = buf(n % 2)
            put(n, total(v[0], v))

        loop(0, count, one)

    def put_a(n, v):
        p1a[n // 2, span(2 * (n % 2), 2, 2)] = v

    def put_b(n, v):
        p1b[n // 2, n % 2] = v

    def put_c(n, v):
        p1c[span(2 * n, 2, 2)] = v

    first_sum(0, 4, r1a, lambda s, n: r1a.at[s, n // 2, span(2 * (n % 2), 2, 2)], lambda i: la.at[i, :, :, :, :RA], put_a)
    s2a = go(by_y(lambda v: p1a.at[:, v], lambda d: r2a.at[d], 0))
    first_sum(1, 4, r1b, lambda s, n: r1b.at[s, n // 2, n % 2], lambda i: lb.at[i, :, :, :RB], put_b)
    s2b = go(by_z(lambda zlv, zhv: p1b.at[zlv, zhv], lambda d: r2b.at[d], 1))
    first_sum(2, 2, r1c, lambda s, n: r1c.at[s, span(2 * n, 2, 2)], lambda i: lc.at[i], put_c)
    s2c = go(by_x(lambda v: p1c.at[:, v], lambda d: r2c.at[d], 2))

    def core_go(b, gv):
        gs[b] = gv.astype(BF16).reshape(8, 64, D)
        return go([rdma(gs.at[b, :, span(32 * (1 - c), 32, 32)], cr.at[b], gsem.at[0, 3, b], gsem.at[1, 3, b], core)])

    s_core = core_go(3, dot_tn(ob[...], gab[...]))
    loop(1, 4, lambda i: attend_back(i, qkv, pb, cag))

    for b in range(3):
        s_core += core_go(b, dot(h1t[...], cag[:ROWS, D * b : D * b + D] if b < 2 else cag[ROWS:, :D]))

    arrived(s2a)
    p2a[...] = total(p1a[:, y], r2a)
    s3a = go(by_z(lambda zlv, zhv: p2a.at[zlv, zhv], lambda d: r3a.at[d], 4))
    arrived(s2b)
    p2b[...] = total(p1b[zl, zh], r2b)
    s3b = go(by_x(lambda v: p2b.at[v], lambda d: r3b.at[d], 5))
    arrived(s2c)
    p2c[...] = total(p1c[:, x], r2c)
    s3c = go(by_y(lambda v: p2c.at[v], lambda d: r3c.at[d], 6))

    arrived(s_core)

    def core_sum(j):
        mine = gs[:, j, span(32 * c, 32, 32)]
        gc[:, j // 4, j % 4] = (mine.astype(F32) + cr[:, j].astype(F32)).astype(BF16)

    loop(0, 8, core_sum)
    t1a = go(by_x(lambda v: gc.at[v, :, :, 0:16], lambda d: qa1.at[d], 7))
    t1b = go(by_z(lambda zlv, zhv: gc.at[span(2 * zhv, 2, 2), zlv, :, 16:32], lambda d: qb1.at[d], 8))

    last = lambda i: first_norm_back(i, tok, cot, aux, s_ref, mt, cag, x1, vec, gt)
    loop(0, 2, last)

    arrived(s3a)
    fp[:RA] = total(p2a[zl, zh], r3a)
    arrived(s3b)
    fp[RA : RA + RB] = total(p2b[x], r3b)
    arrived(s3c)
    fp[RA + RB :] = total(p2c[y], r3c)
    f_own = pltpu.make_async_copy(fp, f_all.at[c, zh, x], lsem.at[0])
    f_own.start()
    f_z = go([rdma(fp, f_all.at[c, zh, x], gsem.at[0, 9, 1], gsem.at[1, 9, 1], dev(zh_=1 - zh))])

    loop(2, IMG, last)
    m_x.wait_recv()
    loop(0, IMG, lambda i: layer_result(i, tok, aux, m, mr, out))

    mr_g = dot_tn(glb[...], h2[:ROWS])
    row = lax.broadcasted_iota(jnp.int32, (8, D), 0)
    mx[0, c] = jnp.where(row < 4, mr_g[:8], vec[...])

    def misc_go(n, me, targets):
        return go([rdma(mx.at[n, me], mx.at[n, me], msem.at[0, n, d], msem.at[1, n, d], t) for d, t in targets])

    def misc_sum(n, count):
        acc = mx[n, 0]
        for i in range(1, count):
            acc = acc + mx[n, i]
        return acc

    m0 = misc_go(0, c, [(1, core)])

    f_own.wait()
    arrived(f_z)
    f_x = go(by_x(lambda v: f_all.at[c, :, x], lambda d: f_all.at[c, :, x], 12))

    arrived(t1b)
    gb2[...] = total(gc[span(2 * zh, 2, 2), zl, :, 16:32], qb1)
    t2b = go(by_x(lambda v: gb2.at[v // 2, :, :, span(256 * (v % 2), 256, 256)], lambda d: qb2.at[d], 11))
    arrived(t1a)
    ga2[...] = total(gc[x, :, :, 0:16], qa1)
    t2a = go(by_y(lambda v: ga2.at[:, v], lambda d: qa2.at[d], 10))

    arrived(m0)
    mx[1, x] = misc_sum(0, 2)
    m1 = misc_go(1, x, [(d, dev(x_=up(x, d))) for d in (1, 2, 3)])

    arrived(t2a)
    ga3[...] = total(ga2[:, y], qa2)
    t3a = go(by_z(lambda zlv, zhv: ga3.at[zlv, :, span(256 * zhv, 256, 256)], lambda d: qa3.at[d], 13))
    arrived(t2b)
    gb3[...] = total(gb2[x // 2, :, :, span(256 * (x % 2), 256, 256)], qb2)
    t3b = go(by_y(lambda v: gb3.at[v], lambda d: qb3.at[d], 14))

    arrived(m1)
    mx[2, y] = misc_sum(1, 4)
    m2 = misc_go(2, y, [(d, dev(y_=up(y, d))) for d in (1, 2, 3)])

    me = c * 8 + zh * 4 + x
    arrived(t3a)
    sf[me, 0] = total(ga3[zl, :, span(256 * zh, 256, 256)], qa3)
    arrived(t3b)
    sf[me, 1] = total(gb3[y], qb3)
    t4 = []
    for d in range(1, 16):
        target = dev(c_=(c + d // 8) % 2, zh_=(zh + d // 4) % 2, x_=up(x, d % 4))
        t4.append(rdma(sf.at[me], sf.at[me], bsem.at[0, d], bsem.at[1, d], target))
    go(t4)

    arrived(m2)
    mx[3, z] = misc_sum(2, 4)
    m3 = misc_go(3, z, [(d, dev_z(up(z, d))) for d in (1, 2, 3)])
    arrived(f_x)
    f_c = go([rdma(f_all.at[c], f_all.at[c], gsem.at[0, 15, 1], gsem.at[1, 15, 1], core)])
    arrived(m3)
    misc[...] = misc_sum(3, 4)
    arrived(t4)
    arrived(f_c)

    for cp in started:
        cp.wait_send()
    for cp in [gm_x, gh2_x, gcp_x, m_x]:
        cp.wait_send()
    loop(0, IMG, lambda i: (h2_x(i).wait_send(), comb_x(i).wait_send()))
    for d in (1, 2, 3):
        v_y(d).wait_send()
        for n in range(3):
            w_x(n, d).wait_send()
    for d, h in all_w_y:
        w_y(d, h).wait_send()
    for way, d, h in all_w_z:
        w_z(way, d, h).wait_send()
    for d in range(4):
        v_z(d).wait_send()
        for p in (0, 1):
            if d:
                s_y(p, d).wait_send()
            for way in (0, 1):
                s_z(p, way, d).wait_send()
            for dz in (0, 1):
                if (dz, d) != (0, 0):
                    s_c(p, dz, d).wait_send()


def finish(f_ref, sf_ref, gin, gout, gq, ga):
    for k in range(2):
        w = slice(128 * k, 128 * k + 128)
        gin[0, :, w] = f_ref[k, 0].astype(F32)
        gout[0, w, :] = jnp.transpose(f_ref[k, 1].astype(F32))
    for k in range(2):
        for zh in range(2):
            for x in range(4):
                for p, lanes in ((0, 512 * x + 256 * zh), (1, 1024 * zh + 256 * x)):
                    rows = slice(32 * k + 16 * p, 32 * k + 16 * p + 16)
                    v = sf_ref[k * 8 + zh * 4 + x, p].astype(F32)
                    if lanes < 3 * D:
                        gq[rows, lanes : lanes + 256] = v
                    else:
                        ga[rows, lanes - 3 * D : lanes - 3 * D + 256] = v


def per_device(
    tokens, key_mask, image_live, routes, ln1_gain, ln1_bias, w_qkv, w_attn, ln2_gain, ln2_bias,
    w_router, w_in, w_out, cotangent,
):
    images, length, width = tokens.shape
    rows8 = jnp.concatenate(
        [w_router.T, ln1_gain[None], ln1_bias[None], ln2_gain[None], ln2_bias[None], jnp.zeros((8, 64), BF16)], axis=0
    )
    odd = lax.axis_index("fsdp") % 2
    v_in = jnp.concatenate([jnp.where(odd == 0, rows8, 0), jnp.where(odd == 1, rows8, 0)], axis=1)
    bias = jnp.where(key_mask > 0, 0.0, NEG).astype(F32)[:, None, :]
    live = jnp.broadcast_to(image_live.astype(F32)[:, None, None], (images, 1, length))
    prep = jnp.concatenate([routes.transpose(0, 2, 1).astype(F32), bias, live, jnp.zeros((images, 4, length), F32)], axis=1)
    tail = jnp.where(jnp.arange(8) == 2, NEG, 0.0).astype(F32)[None, :, None]
    prep = jnp.concatenate([prep, jnp.broadcast_to(tail, (images, 8, 256 - length))], axis=2)

    sds = jax.ShapeDtypeStruct
    vm = pl.BlockSpec(memory_space=pltpu.VMEM)
    hbm = pl.BlockSpec(memory_space=pl.ANY)
    V = pltpu.VMEM
    S = pltpu.SemaphoreType.DMA
    outs = pl.pallas_call(
        kernel,
        in_specs=[vm, vm, vm, hbm, hbm, hbm, hbm, hbm],
        out_specs=[vm, vm, vm, vm, hbm, hbm, hbm, hbm, hbm],
        out_shape=[
            sds((IMG, LEN, D), BF16),
            sds((IMG, LEN, D), F32),
            sds((16, 2, 16, 256), BF16),
            sds((8, D), F32),
            sds((8, 2 * CH, D), BF16),
            sds((2, 2, 4, 128, CH), BF16),
            sds((4, 2, 4, 2, RA, CH), BF16),
            sds((4, 2, 2, 4, RB, CH), BF16),
            sds((4, 4, 4, RC, CH), BF16),
        ],
        scratch_shapes=[
            V((D, 2048), BF16),
            V((2, 2 * CH, D), BF16),
            V((2, 2, 4, 128, CH), BF16),
            V((ROWS, D), BF16),
            V((D, ROWS), BF16),
            V((ROWS, 3 * D), BF16),
            V((IMG * HEADS, PAD, PAD), BF16),
            V((ROWS, D), BF16),
            V((ROWS, D), F32),
            V((PAIR, D), BF16),
            V((PAIR, D), BF16),
            V((D, PAIR), BF16),
            V((D, PAIR), BF16),
            V((ROWS, 128), F32),
            V((PAIR, 128), BF16),
            V((PAIR, CH), BF16),
            V((PAIR, D), F32),
            V((PAIR, D), F32),
            V((PAIR, CH), F32),
            V((PAIR, 2 * CH), BF16),
            V((ROWS, D), BF16),
            V((ROWS, D), BF16),
            V((ROWS, 128), F32),
            V((ROWS, 128), F32),
            V((8, D), F32),
            V((8, D), F32),
            V((4, 4, 8, D), F32),
            V((ROWS, 128), BF16),
            V((8, 16, 128), BF16),
            V((128, D), BF16),
            V((4, 8, 32, 512), BF16),
            V((4, 2, 4, 32, 512), BF16),
            V((4, 2, 4, 16, 512), BF16),
            V((4, 2, 4, 16, 512), BF16),
            V((4, 2, 16, 512), BF16),
            V((4, 4, 16, 256), BF16),
            V((4, 16, 256), BF16),
            V((4, 16, 256), BF16),
            V((2, 4, 16, 512), BF16),
            V((2, 4, 16, 512), BF16),
            V((2, 16, 512), BF16),
            V((4, 16, 256), BF16),
            V((4, 2, 2, RA, CH), BF16),
            V((4, 4, RB, CH), BF16),
            V((4, 4, RC, CH), BF16),
            V((4, RA, CH), BF16),
            V((4, RB, CH), BF16),
            V((4, RC, CH), BF16),
            S((11,)),
            S((2, 2, 4)),
            S((2, 2, 2, 4)),
            S((2, 2, 2, 4)),
            S((2, 4)),
            S((2, 4)),
            S((2, 8)),
            S((2, 3, 4)),
            S((2, 2, 8)),
            S((2, 12)),
            S((2, 6)),
            S((2, 3)),
            S((3, 4)),
            S((2, 4)),
            S((2, 16, 4)),
            S((2, 4, 4)),
            S((2,)),
            S((2, 16)),
        ],
        compiler_params=pltpu.CompilerParams(
            collective_id=0, has_side_effects=True, vmem_limit_bytes=61 * 1024 * 1024
        ),
        cost_estimate=pl.CostEstimate(flops=50_000_000_000, bytes_accessed=60_000_000, transcendentals=10_000_000),
        name="layer",
    )(tokens, prep, cotangent, w_qkv, w_attn, v_in, w_in, w_out)
    layer_out, grad_tokens, sf, misc, _, f_all = outs[:6]
    g_in, g_out, g_qkv, g_attn = pl.pallas_call(
        finish,
        grid=(4,),
        in_specs=[
            pl.BlockSpec((2, 2, D, 128), lambda e: (0, 0, 0, e)),
            pl.BlockSpec((16, 2, 16, 256), lambda e: (0, 0, 0, 0)),
        ],
        out_specs=[
            pl.BlockSpec((1, D, 256), lambda e: (e, 0, 0)),
            pl.BlockSpec((1, 256, D), lambda e: (e, 0, 0)),
            pl.BlockSpec((64, 3 * D), lambda e: (0, 0)),
            pl.BlockSpec((64, D), lambda e: (0, 0)),
        ],
        out_shape=[sds((4, D, 256), F32), sds((4, 256, D), F32), sds((64, 3 * D), F32), sds((64, D), F32)],
        name="finish",
    )(f_all.reshape(2, 2, D, CH), sf)
    mine = lax.dynamic_slice(misc, (0, 64 * lax.axis_index("fsdp")), (8, 64))
    return (layer_out, grad_tokens, mine[4], mine[5], g_qkv, g_attn, mine[6], mine[7], mine[:4].T, g_in, g_out)


def solution(mesh):
    dev = ("dp", "fsdp", "seq")
    in_specs = (
        P(dev, None, None), P(dev, None), P(dev), P(dev, None, None), P("fsdp"), P("fsdp"), P("fsdp", None),
        P("fsdp", None), P("fsdp"), P("fsdp"), P("fsdp", None), P(None, None, "fsdp"), P(None, "fsdp", None),
        P(dev, None, None),
    )
    out_specs = (
        P(dev, None, None), P(dev, None, None), P("fsdp"), P("fsdp"), P("fsdp", None), P("fsdp", None), P("fsdp"),
        P("fsdp"), P("fsdp", None), P(None, None, "fsdp"), P(None, "fsdp", None),
    )
    return jax.shard_map(per_device, mesh=mesh, in_specs=in_specs, out_specs=out_specs, check_vma=False)
```

```python
import jax
import jax.numpy as jnp
from jax import lax
from jax.experimental import pallas as pl
from jax.experimental.pallas import tpu as pltpu
from jax.sharding import PartitionSpec as P

F32 = jnp.float32
BF16 = jnp.bfloat16
MESH = pl.DeviceIdType.MESH
HEADS = 8
EPS = 1e-06
NEG = -1000000000.0
D = 512
IMG = 4
LEN = 200
PAD = 208
ROWS = IMG * PAD
PAIR = 2 * ROWS
HD = 64
CH = 512
TM = 832
RA, RB, RC = 48, 48, 32


def dot(a, b):
    return jnp.dot(a, b, preferred_element_type=F32)


def dot_nt(a, b):
    return lax.dot_general(a, b, (((1,), (1,)), ((), ())), preferred_element_type=F32)


def dot_tn(a, b):
    return lax.dot_general(a, b, (((0,), (0,)), ((), ())), preferred_element_type=F32)


def rows_of(i):
    return pl.ds(pl.multiple_of(i * PAD, 16), PAD)


def span(start, size, unit):
    return pl.ds(pl.multiple_of(start, unit), size)


def pad_rows(v):
    return jnp.concatenate([v, jnp.zeros((PAD - LEN, v.shape[1]), v.dtype)], axis=0)


def normalize(v):
    c = v - jnp.mean(v, axis=-1, keepdims=True)
    r = lax.rsqrt(jnp.mean(c * c, axis=-1, keepdims=True) + EPS)
    return c * r, r


def lane(shape):
    return lax.broadcasted_iota(jnp.int32, shape, 1)


def loop(lo, hi, body):
    def step(i, carry):
        body(i)
        return carry

    lax.fori_loop(lo, hi, step, 0)


def norm_back(u, n, r):
    return r * (u - jnp.mean(u, axis=-1, keepdims=True) - n * jnp.mean(u * n, axis=-1, keepdims=True))


def ln_one(tok, mt, h1):
    def body(i):
        n, _ = normalize(pad_rows(tok[i].astype(F32)))
        h1[rows_of(i)] = (n * mt[4:5] + mt[5:6]).astype(BF16)

    loop(0, IMG, body)


def make_qkv(s_ref, h1, qkv):
    for b in range(3):
        v = dot(h1[...], s_ref[:, D * b : D * b + D]).astype(BF16)
        if b == 0:
            v = v * jnp.asarray(HD**-0.5, BF16)
        qkv[:, D * b : D * b + D] = v


def attend(i, qkv, prep, pb, ob):
    r = rows_of(i)
    bias = prep[i, 2:3, :PAD]
    low = lane((PAD, 128)) < HD
    for hp in range(HEADS // 2):
        o = 128 * hp
        q2, k2, v2 = qkv[r, o : o + 128], qkv[r, D + o : D + o + 128], qkv[r, 2 * D + o : 2 * D + o + 128]
        outs = []
        for a in range(2):
            qm = jnp.where(low if a == 0 else ~low, q2, jnp.zeros_like(q2))
            s = dot_nt(qm, k2) + bias
            e = jnp.exp(s - jnp.max(s, axis=-1, keepdims=True))
            p = (e * (1.0 / jnp.sum(e, axis=-1, keepdims=True))).astype(BF16)
            pb[i * HEADS + hp * 2 + a] = p
            outs.append(dot(p, v2))
        ob[r, o : o + 128] = jnp.where(low, outs[0], outs[1]).astype(BF16)


def middle(i, tok, s_ref, mt, mtb, ob, aux, x1, h2, gates, comb):
    r = rows_of(i)
    v = pad_rows(tok[i].astype(F32)) + dot(ob[r], s_ref[:, 3 * D :])
    x1[r] = v
    n, _ = normalize(v)
    h = (n * mt[6:7] + mt[7:8]).astype(BF16)
    h2[r] = h
    lg = dot_nt(h, mtb[...])
    ok = lane((PAD, 128)) < 4
    lg = jnp.where(ok, lg, -1e30)
    e = jnp.exp(lg - jnp.max(lg, axis=-1, keepdims=True))
    g = e / jnp.sum(e, axis=-1, keepdims=True)
    gates[r] = g
    comb[r] = jnp.where(ok, g * aux[r].astype(F32), 0.0).astype(BF16)


def masks(i, prep, aux):
    row = lax.broadcasted_iota(jnp.int32, (128, 256), 0)
    v = prep[i]
    e = row.astype(F32)
    hit = ((v[0:1] == e) | (v[1:2] == e)) & (row < 4)
    flags = jnp.where(hit, 1.0, jnp.where(row == 4, v[3:4], 0.0))
    aux[rows_of(i)] = jnp.transpose(flags)[:PAD].astype(BF16)


def live_cotangent(i, cot, aux, gm):
    r = rows_of(i)
    gm[r] = (pad_rows(cot[i].astype(F32)) * aux[r, 4:5].astype(F32)).astype(BF16)


def expander():
    return (
        lax.broadcasted_iota(jnp.int32, (128, CH), 0) == lax.broadcasted_iota(jnp.int32, (128, CH), 1) // 128
    ).astype(BF16)


def experts_tile(lo, w, h2, gm, cx, gca, m, gh2, cag):
    r = pl.ds(lo, TM)
    win, wout = w[:CH], w[CH:]
    hid = dot(h2[r], win)
    ga = dot_nt(gm[r], wout)
    cdf = 0.5 * (1.0 + lax.erf(hid * 0.7071067811865476))
    slope = cdf + hid * jnp.exp(-0.5 * hid * hid) * 0.3989422804014327
    act = hid * cdf
    c = cx[r].astype(F32)
    gca[r] += act * ga
    ca = (act * c).astype(BF16)
    gh = (ga * c * slope).astype(BF16)
    cag[r, :CH] = ca
    cag[r, CH:] = gh
    m[r] += dot(ca, wout)
    gh2[r] += dot_nt(gh, win)


def layer_result(i, tok, aux, m, mr, out):
    r = rows_of(i)
    v = m[r] + mr[r].astype(F32)
    out[i] = jnp.where(aux[r, 4:5].astype(F32) > 0, v, pad_rows(tok[i].astype(F32)))[:LEN].astype(BF16)


def second_norm_back(i, mtb, mt, aux, gates, gca, gcr, gh2, gh2r, gm, x1, m, glb, gab, vec):
    r = rows_of(i)
    ok = lane((PAD, 128)) < 4
    ch = jnp.where(ok, aux[r].astype(F32), 0.0)
    g = gates[r]
    gg = (dot_nt(gca[r].astype(BF16), expander()) + gcr[r]) * ch
    gl = (g * (gg - jnp.sum(gg * g, axis=-1, keepdims=True))).astype(BF16)
    glb[r] = gl
    gh = gh2[r] + gh2r[r].astype(F32) + dot(gl, mtb[...])
    n, r2 = normalize(x1[r])
    vec[6:7] += jnp.sum(gh * n, axis=0, keepdims=True)
    vec[7:8] += jnp.sum(gh, axis=0, keepdims=True)
    gx = gm[r].astype(F32) + norm_back(gh * mt[6:7], n, r2)
    m[r] += x1[r]
    x1[r] = gx
    gab[r] = gx.astype(BF16)


def attend_back(i, qkv, pb, cag):
    r = rows_of(i)
    rv = span(ROWS + i * PAD, PAD, 16)
    low = lane((PAD, 128)) < HD
    for hp in range(HEADS // 2):
        o = 128 * hp
        q2, k2, v2 = qkv[r, o : o + 128], qkv[r, D + o : D + o + 128], qkv[r, 2 * D + o : 2 * D + o + 128]
        g2 = cag[rv, D + o : D + o + 128]
        gq, gk, gv = [], [], []
        for a in range(2):
            gmk = jnp.where(low if a == 0 else ~low, g2, jnp.zeros_like(g2))
            p = pb[i * HEADS + hp * 2 + a]
            pf = p.astype(F32)
            t = dot_nt(gmk, v2)
            gs = (pf * (t - jnp.sum(t * pf, axis=-1, keepdims=True))).astype(BF16)
            gq.append(dot(gs, k2))
            gk.append(dot_tn(gs, q2))
            gv.append(dot_tn(p, g2))
        cag[r, o : o + 128] = (jnp.where(low, gq[0], gq[1]) * HD**-0.5).astype(BF16)
        cag[r, D + o : D + o + 128] = jnp.where(low, gk[0], gk[1]).astype(BF16)
        cag[rv, o : o + 128] = jnp.where(low, gv[0], gv[1]).astype(BF16)


def first_norm_back(i, tok, cot, aux, s_ref, mt, cag, x1, vec, gt):
    r = rows_of(i)
    rv = span(ROWS + i * PAD, PAD, 16)
    gh = (
        dot_nt(cag[r, :D], s_ref[:, :D])
        + dot_nt(cag[r, D:], s_ref[:, D : 2 * D])
        + dot_nt(cag[rv, :D], s_ref[:, 2 * D : 3 * D])
    )
    n, r1 = normalize(pad_rows(tok[i].astype(F32)))
    vec[4:5] += jnp.sum(gh * n, axis=0, keepdims=True)
    vec[5:6] += jnp.sum(gh, axis=0, keepdims=True)
    gd = jnp.where(aux[r, 4:5].astype(F32) > 0, 0.0, pad_rows(cot[i].astype(F32)))
    gt[i] = (gd + x1[r] + norm_back(gh * mt[4:5], n, r1))[:LEN]


def order(k):
    dy = jnp.where((k == 1) | (k == 4), 2, jnp.where((k == 2) | (k == 5), 1, jnp.where((k == 3) | (k == 6), 3, 0)))
    dz = jnp.where(k >= 4, 1, 0)
    return dz, dy


def kernel(
    tok, prep, cot, q_in, a_in, v_in, w_in, w_out,
    out, gt, sf, misc, w_all, f_all, r1a, r1b, r1c,
    s_ref, wbuf, gst, h1, h1t, qkv, pb, ob, x1, h2, gm, h2t, gmt, gates, comb, cx, m, gh2, gca, cag,
    gh2r, mr, gcp, gcr, mt, vec, mx, aux, mtg, mtb,
    cr, gc, qa1, qb1, qa2, qb2, qa3, qb3, ga2, gb2, ga3, gb3, r2a, r2b, r2c,
    r3a, r3b, r3c,
    lsem, sy, sz, sc, vy, vz, wy, wx, wz, px, ssem, lsem2, rsem, asem, gsem, msem, wsem, bsem,
):
    zh, f, sq = lax.axis_index("dp"), lax.axis_index("fsdp"), lax.axis_index("seq")
    zl, y = f // 4, f % 4
    x, c = sq // 2, sq % 2
    z = zh * 2 + zl

    def dev(zh_=zh, zl_=zl, y_=y, x_=x, c_=c):
        return (zh_, zl_ * 4 + y_, x_ * 2 + c_)

    def up(v, d):
        return (v + d) % 4

    def dev_z(zz):
        return dev(zh_=zz // 2, zl_=zz % 2)

    core = dev(c_=1 - c)

    def rdma(src, dst, ssm, rsm, target):
        return pltpu.make_async_remote_copy(
            src_ref=src, dst_ref=dst, send_sem=ssm, recv_sem=rsm, device_id=target, device_id_type=MESH
        )

    barrier = pltpu.get_barrier_semaphore()
    for d in (1, 2, 3):
        for target in (dev(x_=up(x, d)), dev(y_=up(y, d)), dev_z(up(z, d))):
            pl.semaphore_signal(barrier, inc=1, device_id=target, device_id_type=MESH)
    others = [(1, 0, 0)] + [(dc, dzh, d) for dc in (0, 1) for dzh in (0, 1) for d in range(4) if d and dc + dzh]
    others += [(1, 1, 0)]
    for dc, dzh, d in others:
        target = dev(c_=(c + dc) % 2, zh_=(zh + dzh) % 2, x_=up(x, d))
        pl.semaphore_signal(barrier, inc=1, device_id=target, device_id_type=MESH)

    own = [
        pltpu.make_async_copy(q_in, s_ref.at[span(64 * f, 64, 64), : 3 * D], lsem.at[0]),
        pltpu.make_async_copy(a_in, s_ref.at[span(64 * f, 64, 64), 3 * D :], lsem.at[9]),
        pltpu.make_async_copy(v_in, mtg.at[f], lsem.at[10]),
    ]
    half = span(128 * c, 128, 128)
    for e in range(4):
        own.append(
            pltpu.make_async_copy(w_in.at[e, :, half], wbuf.at[0, :CH, 128 * e : 128 * e + 128], lsem.at[1 + e])
        )
        own.append(
            pltpu.make_async_copy(w_out.at[e, half, :], wbuf.at[0, CH + 128 * e : CH + 128 * e + 128], lsem.at[5 + e])
        )
    for cp in own:
        cp.start()
    pl.semaphore_wait(barrier, 9 + len(others))
    for cp in own[:3]:
        cp.wait()

    cols = (slice(0, 3 * D), slice(3 * D, 4 * D))

    def s_part(p, zz, yy, cc, size=32, off=0):
        return s_ref.at[span((zz * 4 + yy) * 64 + 32 * cc + off, size, 16), cols[p]]

    def s_y(p, d):
        r = s_part(p, zl, y, c)
        return rdma(r, r, sy.at[0, p, d], sy.at[1, p, d], dev(y_=up(y, d)))

    def s_z(p, way, d):
        r = s_part(p, zl, up(y, 4 - d), c, 16, 16 * way)
        return rdma(r, r, sz.at[0, p, way, d], sz.at[1, p, way, d], dev_z(up(z, 1 if way == 0 else 3)))

    def s_c(p, dz, d):
        r = s_part(p, (zl + dz) % 2, up(y, 4 - d), c)
        return rdma(r, r, sc.at[0, p, dz, d], sc.at[1, p, dz, d], core)

    def v_y(d):
        return rdma(mtg.at[f], mtg.at[f], vy.at[0, d], vy.at[1, d], dev(y_=up(y, d)))

    def v_z(d):
        r = mtg.at[zl * 4 + up(y, 4 - d)]
        return rdma(r, r, vz.at[0, d], vz.at[1, d], dev_z(up(z, 1)))

    def s_z_done(p):
        for d in (0, 1, 3, 2):
            for way in (0, 1):
                s_z(p, way, d).wait_recv()
            s_c(p, 1, d).start()

    def s_c_done(p):
        for dz in (0, 1):
            for d in range(4):
                if (dz, d) != (0, 0):
                    s_c(p, dz, d).wait_recv()

    for d in (1, 3, 2):
        v_y(d).start()
    v_z(0).start()
    for p in (0, 1):
        for d in (1, 3, 2):
            s_y(p, d).start()
        for way in (0, 1):
            s_z(p, way, 0).start()

    loop(0, IMG, lambda i: (masks(i, prep, aux), live_cotangent(i, cot, aux, gm)))
    own_rows, peer_rows = pl.ds(0, ROWS), pl.ds(ROWS, ROWS)
    gm_x = rdma(gm.at[own_rows], gm.at[peer_rows], px.at[0, 0], px.at[1, 0], core)

    for d in (1, 3, 2):
        v_y(d).wait_recv()
        v_z(d).start()
    for p in (0, 1):
        for d in (1, 3, 2):
            s_y(p, d).wait_recv()
            for way in (0, 1):
                s_z(p, way, d).start()
            s_c(p, 0, d).start()

    def w_y(d, h=0):
        r = w_all.at[f, span(256 * x, 256, 256)] if d == 2 else w_all.at[f, CH * h : CH * h + CH]
        return rdma(r, r, wy.at[0, d + 4 * h], wy.at[1, d + 4 * h], dev(y_=up(y, d)))

    def w_x(n, d):
        dz, dy = ((0, 2), (1, 0), (1, 2))[n]
        r = w_all.at[((zl + dz) % 2) * 4 + up(y, dy), span(256 * x, 256, 256)]
        return rdma(r, r, wx.at[0, n, d], wx.at[1, n, d], dev(x_=up(x, d)))

    def w_z(way, d, h=0):
        chunk_of = w_all.at[zl * 4 + up(y, 4 - d)]
        if d % 2 == 0:
            r = chunk_of.at[span(256 * x + 128 * way, 128, 128)]
        else:
            r = chunk_of.at[CH * h + 256 * way : CH * h + 256 * way + 256]
        return rdma(r, r, wz.at[0, way, d + 4 * h], wz.at[1, way, d + 4 * h], dev_z(up(z, 1 if way == 0 else 3)))

    all_w_y = [(2, 0), (1, 0), (3, 0), (1, 1), (3, 1)]
    all_w_z = [(way, d, h) for d, h in [(0, 0), (2, 0), (1, 0), (3, 0), (1, 1), (3, 1)] for way in (0, 1)]

    for cp in own[3:]:
        cp.wait()
    w_own = pltpu.make_async_copy(wbuf.at[0], w_all.at[f], lsem.at[0])
    w_own.start()
    w_own.wait()
    for d, h in all_w_y[:3]:
        w_y(d, h).start()

    gm_x.start()
    gmt[:, :ROWS] = gm[:ROWS].T
    for d in range(4):
        v_z(d).wait_recv()
    mt[...] = jnp.concatenate([(mtg[2 * i, :8] + mtg[2 * i + 1, :8]).astype(F32) for i in range(4)], axis=1)
    mtb[...] = jnp.concatenate([mt[...], jnp.zeros((120, D), F32)], axis=0).astype(BF16)
    vec[...] = jnp.zeros_like(vec)
    s_z_done(0)
    for way in (0, 1):
        w_z(way, 0).start()
    ln_one(tok, mt, h1)
    s_c_done(0)

    make_qkv(s_ref, h1, qkv)
    s_z_done(1)
    w_y(2).wait_recv()
    for d in (1, 2, 3):
        w_x(0, d).start()
    for way in (0, 1):
        w_z(way, 2).start()
    for way in (0, 1):
        w_z(way, 0).wait_recv()
    for d in (1, 2, 3):
        w_x(1, d).start()
    s_c_done(1)

    def h2_x(i):
        return rdma(h2.at[rows_of(i)], h2.at[span(ROWS + i * PAD, PAD, 16)], px.at[0, 3 + i], px.at[1, 3 + i], core)

    def comb_x(i):
        return rdma(comb.at[rows_of(i)], comb.at[span(ROWS + i * PAD, PAD, 16)], px.at[0, 7 + i], px.at[1, 7 + i], core)

    def forward(i):
        attend(i, qkv, prep, pb, ob)
        middle(i, tok, s_ref, mt, mtb, ob, aux, x1, h2, gates, comb)
        h2_x(i).start()
        comb_x(i).start()

    loop(0, 2, forward)
    for d in (1, 3):
        w_y(d, 0).wait_recv()
        w_y(d, 1).start()
        for way in (0, 1):
            w_z(way, d, 0).start()
    loop(2, IMG, forward)
    for way in (0, 1):
        w_z(way, 2).wait_recv()
    for d in (1, 2, 3):
        w_x(2, d).start()
    gm_x.wait_recv()
    gmt[:, ROWS:] = gm[ROWS:].T
    h1t[...] = h1[...].T
    h2t[:, :ROWS] = h2[:ROWS].T

    def load_w(k):
        dz, dy = order(k)
        return pltpu.make_async_copy(w_all.at[((zl + dz) % 2) * 4 + up(y, 4 - dy)], wbuf.at[k % 2], wsem.at[k % 2])

    m[...] = jnp.zeros_like(m)
    gh2[...] = jnp.zeros_like(gh2)
    gca[...] = jnp.zeros_like(gca)
    ex = expander()
    cx[:ROWS] = dot(comb[:ROWS], ex).astype(BF16)
    loop(0, IMG, lambda i: (h2_x(i).wait_recv(), comb_x(i).wait_recv()))
    h2t[:, ROWS:] = h2[ROWS:].T
    cx[ROWS:] = dot(comb[ROWS:], ex).astype(BF16)

    def sends(k, act):
        slot = k % 2
        dz, dy = order(k)
        zz, yy = (zl + dz) % 2, up(y, 4 - dy)

        def local(src, dst, i):
            cp = pltpu.make_async_copy(src, dst, lsem2.at[slot, i])
            cp.start() if act == 0 else cp.wait()

        def remote(src, dst, i, rsm, target):
            cp = rdma(src, dst, ssem.at[slot, i], rsm, target)
            cp.start() if act == 0 else cp.wait_send()

        g = gst.at[slot]
        for d in (1, 2, 3):
            remote(g.at[:, up(x, d), :RA], r1a.at[d, zz, yy], d - 1, rsem.at[0, d], dev(x_=up(x, d)))
        local(g.at[:, x, :RA], r1a.at[0, zz, yy], 0)

        @pl.when(dy != 0)
        def _():
            remote(g.at[:, :, RA : RA + RB], r1b.at[dy, zz], 3, rsem.at[1, dy], dev(y_=yy))

        @pl.when(dy == 0)
        def _():
            local(g.at[:, :, RA : RA + RB], r1b.at[0, zz], 1)

        remote(g.at[1 - zh, :, RA + RB :], r1c.at[2 + dz, yy], 4, rsem.at[2, 2 + dz], dev(zh_=1 - zh, zl_=zz))

        @pl.when(dz != 0)
        def _():
            remote(g.at[zh, :, RA + RB :], r1c.at[1, yy], 5, rsem.at[2, 1], dev(zl_=zz))

        @pl.when(dz == 0)
        def _():
            local(g.at[zh, :, RA + RB :], r1c.at[0, yy], 2)

    gh2_x = rdma(cx.at[peer_rows], gh2r, px.at[0, 1], px.at[1, 1], core)
    gcp_x = rdma(gcp, gcr, px.at[0, 2], px.at[1, 2], core)
    m_x = rdma(h1, mr, px.at[0, 11], px.at[1, 11], core)

    def chunk(k):
        slot = k % 2
        w = wbuf.at[slot]
        experts_tile(ROWS, w, h2, gm, cx, gca, m, gh2, cag)

        @pl.when(k < 7)
        def _():
            nxt = k + 1

            for n, part in ((1, 0), (4, 2), (7, 1)):

                @pl.when(nxt == n)
                def _(part=part):
                    for d in (1, 2, 3):
                        w_x(part, d).wait_recv()

            @pl.when(nxt == 2)
            def _():
                for d in (1, 3):
                    w_y(d, 1).wait_recv()
                    for way in (0, 1):
                        w_z(way, d, 1).start()

            for n, d in ((5, 1), (6, 3)):

                @pl.when(nxt == n)
                def _(d=d):
                    for h in (0, 1):
                        for way in (0, 1):
                            w_z(way, d, h).wait_recv()

            load_w(nxt).start()

        @pl.when(k == 7)
        def _():
            cx[ROWS:] = gh2[ROWS:].astype(BF16)
            gh2_x.start()
            gcp[...] = dot_nt(gca[ROWS:].astype(BF16), expander())
            gcp_x.start()
            h1[...] = m[ROWS:].astype(BF16)
            m_x.start()

        experts_tile(0, w, h2, gm, cx, gca, m, gh2, cag)

        @pl.when(k >= 2)
        def _():
            sends(k - 2, 1)

        for b in range(2):
            gv = dot((h2t if b == 0 else gmt)[...], cag[:, (CH if b == 0 else 0) : (2 * CH if b == 0 else CH)])
            gst[slot, b] = gv.astype(BF16).reshape(4, 128, CH)
        sends(k, 0)

        @pl.when(k < 7)
        def _():
            load_w(k + 1).wait()

    loop(0, 8, chunk)

    glb, gab = comb.at[peer_rows], gm.at[peer_rows]
    flat = wbuf.reshape(4 * CH, D)
    p1a = flat.at[: 16 * RA].reshape(2, 4, 2, RA, CH)
    p1b = flat.at[16 * RA : 16 * (RA + RB)].reshape(2, 2, 4, RB, CH)
    p1c = flat.at[16 * (RA + RB) :].reshape(4, 4, RC, CH)
    gs = gst.reshape(4, 8, 64, D)
    p2a = ob.at[: 4 * RA].reshape(2, 2, RA, CH)
    p2b = ob.at[4 * RA : 4 * (RA + RB)].reshape(4, RB, CH)
    p2c = ob.at[4 * (RA + RB) : 512].reshape(4, RC, CH)
    fp = ob.at[512:640]

    gh2_x.wait_recv()
    gcp_x.wait_recv()
    def second(i):
        second_norm_back(i, mtb, mt, aux, gates, gca, gcr, gh2, gh2r, gm, x1, m, glb, gab, vec)

    loop(0, IMG, second)
    cag[ROWS:, D:] = dot_nt(gab[...], s_ref[:, 3 * D :]).astype(BF16)
    loop(0, 1, lambda i: attend_back(i, qkv, pb, cag))

    started = []

    def go(copies):
        for cp in copies:
            cp.start()
        started.extend(copies)
        return copies

    def arrived(copies):
        for cp in copies:
            cp.wait_recv()

    def by_x(src, dst, n):
        return [
            rdma(src(up(x, d)), dst(d), gsem.at[0, n, d], gsem.at[1, n, d], dev(x_=up(x, d))) for d in (1, 2, 3)
        ]

    def by_y(src, dst, n):
        return [
            rdma(src(up(y, d)), dst(d), gsem.at[0, n, d], gsem.at[1, n, d], dev(y_=up(y, d))) for d in (1, 2, 3)
        ]

    def by_z(src, dst, n):
        copies = []
        for q in (1, 2, 3):
            zhv, zlv = (zh + q // 2) % 2, (zl + q % 2) % 2
            copies.append(rdma(src(zlv, zhv), dst(q), gsem.at[0, n, q], gsem.at[1, n, q], dev(zh_=zhv, zl_=zlv)))
        return copies

    def total(first, rest):
        acc = first.astype(F32)
        for d in (1, 2, 3):
            acc = acc + rest[d].astype(F32)
        return acc.astype(BF16)

    sends(6, 1)
    sends(7, 1)
    for part, recv in enumerate((r1a, r1b, r1c)):
        for d in (1, 2, 3):
            rdma(recv.at[d], recv.at[d], ssem.at[0, 0], rsem.at[part, d], core).wait_recv()

    gh2_x.wait_send()
    room = 16 * RA
    bufs = [gst.reshape(2, 2 * CH, CH).at[i, :room] for i in range(2)] + [cx.at[i * room : i * room + room] for i in range(2)]
    pieces = [((4, 2, 2, RA, CH), lambda s, i=i: r1a.at[s, i // 2, 2 * (i % 2) : 2 * (i % 2) + 2]) for i in range(4)]
    pieces += [((4, 4, RB, CH), lambda s, i=i: r1b.at[s, i // 2, i % 2]) for i in range(4)]
    pieces += [((4, 4, RC, CH), lambda s, i=i: r1c.at[s, i]) for i in range(4)]

    def piece(n):
        shape, src = pieces[n]
        rows = 16 * shape[-2] if len(shape) == 4 else room
        v = bufs[n % 4].at[:rows].reshape(*shape)
        return v, [pltpu.make_async_copy(src(s), v.at[s], asem.at[n % 4, s]) for s in range(4)]

    for n in range(4):
        for cp in piece(n)[1]:
            cp.start()
    for n in range(12):
        v, copies = piece(n)
        for cp in copies:
            cp.wait()
        t = total(v[0], v)
        if n < 4:
            p1a[n // 2, 2 * (n % 2) : 2 * (n % 2) + 2] = t
        elif n < 8:
            p1b[(n - 4) // 2, (n - 4) % 2] = t
        else:
            p1c[n - 8] = t
        if n + 4 < 12:
            for cp in piece(n + 4)[1]:
                cp.start()
        if n == 3:
            s2a = go(by_y(lambda v: p1a.at[:, v], lambda d: r2a.at[d], 0))
        if n == 7:
            s2b = go(by_z(lambda zlv, zhv: p1b.at[zlv, zhv], lambda d: r2b.at[d], 1))
    s2c = go(by_x(lambda v: p1c.at[:, v], lambda d: r2c.at[d], 2))

    def core_go(b, gv):
        gs[b] = gv.astype(BF16).reshape(8, 64, D)
        return go([rdma(gs.at[b, :, span(32 * (1 - c), 32, 32)], cr.at[b], gsem.at[0, 3, b], gsem.at[1, 3, b], core)])

    s_core = core_go(3, dot_tn(ob[...], gab[...]))
    loop(1, 3, lambda i: attend_back(i, qkv, pb, cag))

    arrived(s2a)
    p2a[...] = total(p1a[:, y], r2a)
    s3a = go(by_z(lambda zlv, zhv: p2a.at[zlv, zhv], lambda d: r3a.at[d], 4))
    arrived(s2b)
    p2b[...] = total(p1b[zl, zh], r2b)
    s3b = go(by_x(lambda v: p2b.at[v], lambda d: r3b.at[d], 5))
    arrived(s2c)
    p2c[...] = total(p1c[:, x], r2c)
    s3c = go(by_y(lambda v: p2c.at[v], lambda d: r3c.at[d], 6))

    loop(3, 4, lambda i: attend_back(i, qkv, pb, cag))

    for b in range(3):
        s_core += core_go(b, dot(h1t[...], cag[:ROWS, D * b : D * b + D] if b < 2 else cag[ROWS:, :D]))

    arrived(s3a)
    fp[:RA] = total(p2a[zl, zh], r3a)
    arrived(s3b)
    fp[RA : RA + RB] = total(p2b[x], r3b)
    arrived(s3c)
    fp[RA + RB :] = total(p2c[y], r3c)
    fl, fr = slice(0, 256), slice(256, 512)
    f_own = pltpu.make_async_copy(fp, f_all.at[c, zh, x], lsem.at[0])
    f_own.start()
    across = dev(zh_=1 - zh)
    f_1l = go([rdma(fp.at[:, fl], f_all.at[c, zh, x, :, fl], gsem.at[0, 9, 1], gsem.at[1, 9, 1], across)])
    f_1r = go(by_x(lambda v: fp.at[:, fr], lambda d: f_all.at[c, zh, x, :, fr], 15))

    arrived(s_core)

    def core_sum(j):
        mine = gs[:, j, span(32 * c, 32, 32)]
        gc[:, j // 4, j % 4] = (mine.astype(F32) + cr[:, j].astype(F32)).astype(BF16)

    loop(0, 8, core_sum)
    t1a = go(by_y(lambda v: gc.at[:, :, v, 0:16], lambda d: qa1.at[d], 7))
    t1b = go(by_z(lambda zlv, zhv: gc.at[span(2 * zhv, 2, 2), zlv, :, 16:32], lambda d: qb1.at[d], 8))

    last = lambda i: first_norm_back(i, tok, cot, aux, s_ref, mt, cag, x1, vec, gt)
    loop(0, 2, last)
    f_own.wait()
    arrived(f_1l)
    f_2l = go(by_x(lambda v: f_all.at[c, :, x, :, fl], lambda d: f_all.at[c, :, x, :, fl], 12))
    arrived(f_1r)
    r_part = f_all.at[c, zh, :, :, fr]
    f_2r = go([rdma(r_part, r_part, gsem.at[0, 9, 2], gsem.at[1, 9, 2], across)])
    loop(2, IMG, last)

    mr_g = dot_tn(glb[...], h2[:ROWS])
    row = lax.broadcasted_iota(jnp.int32, (8, D), 0)
    mx[0, c] = jnp.where(row < 4, mr_g[:8], vec[...])

    def misc_go(n, me, targets):
        return go([rdma(mx.at[n, me], mx.at[n, me], msem.at[0, n, d], msem.at[1, n, d], t) for d, t in targets])

    def misc_sum(n, count):
        acc = mx[n, 0]
        for i in range(1, count):
            acc = acc + mx[n, i]
        return acc

    m0 = misc_go(0, c, [(1, core)])

    arrived(t1a)
    ga2[...] = total(gc[:, :, y, 0:16], qa1)
    t2a = go(by_x(lambda v: ga2.at[v], lambda d: qa2.at[d], 10))
    arrived(t1b)
    gb2[...] = total(gc[span(2 * zh, 2, 2), zl, :, 16:32], qb1)
    t2b = go(by_x(lambda v: gb2.at[v // 2, :, :, span(256 * (v % 2), 256, 256)], lambda d: qb2.at[d], 11))

    m_x.wait_recv()
    loop(0, IMG, lambda i: layer_result(i, tok, aux, m, mr, out))

    arrived(m0)
    mx[1, x] = misc_sum(0, 2)
    m1 = misc_go(1, x, [(d, dev(x_=up(x, d))) for d in (1, 2, 3)])

    arrived(t2a)
    ga3[...] = total(ga2[x], qa2)
    t3a = go(by_z(lambda zlv, zhv: ga3.at[zlv, :, span(256 * zhv, 256, 256)], lambda d: qa3.at[d], 13))
    arrived(t2b)
    gb3[...] = total(gb2[x // 2, :, :, span(256 * (x % 2), 256, 256)], qb2)
    t3b = go(by_y(lambda v: gb3.at[v], lambda d: qb3.at[d], 14))

    arrived(m1)
    mx[2, y] = misc_sum(1, 4)
    m2 = misc_go(2, y, [(d, dev(y_=up(y, d))) for d in (1, 2, 3)])

    me = c * 8 + zh * 4 + x
    arrived(t3a)
    sf[me, 0] = total(ga3[zl, :, span(256 * zh, 256, 256)], qa3)
    arrived(t3b)
    sf[me, 1] = total(gb3[y], qb3)
    t4 = []
    for d in range(1, 16):
        target = dev(c_=(c + d // 8) % 2, zh_=(zh + d // 4) % 2, x_=up(x, d % 4))
        t4.append(rdma(sf.at[me], sf.at[me], bsem.at[0, d], bsem.at[1, d], target))
    go(t4)

    arrived(m2)
    mx[3, z] = misc_sum(2, 4)
    m3 = misc_go(3, z, [(d, dev_z(up(z, d))) for d in (1, 2, 3)])
    arrived(f_2l)
    arrived(f_2r)
    f_c = go([rdma(f_all.at[c], f_all.at[c], gsem.at[0, 9, 3], gsem.at[1, 9, 3], core)])
    arrived(m3)
    misc[...] = misc_sum(3, 4)
    arrived(t4)
    arrived(f_c)

    for cp in started:
        cp.wait_send()
    for cp in [gm_x, gcp_x, m_x]:
        cp.wait_send()
    loop(0, IMG, lambda i: (h2_x(i).wait_send(), comb_x(i).wait_send()))
    for d in (1, 2, 3):
        v_y(d).wait_send()
        for n in range(3):
            w_x(n, d).wait_send()
    for d, h in all_w_y:
        w_y(d, h).wait_send()
    for way, d, h in all_w_z:
        w_z(way, d, h).wait_send()
    for d in range(4):
        v_z(d).wait_send()
        for p in (0, 1):
            if d:
                s_y(p, d).wait_send()
            for way in (0, 1):
                s_z(p, way, d).wait_send()
            for dz in (0, 1):
                if (dz, d) != (0, 0):
                    s_c(p, dz, d).wait_send()


def finish(f_ref, sf_ref, gin, gout, gq, ga):
    for k in range(2):
        w = slice(128 * k, 128 * k + 128)
        gin[0, :, w] = f_ref[k, 0].astype(F32)
        gout[0, w, :] = jnp.transpose(f_ref[k, 1].astype(F32))
    for k in range(2):
        for zh in range(2):
            for x in range(4):
                for p, lanes in ((0, 512 * x + 256 * zh), (1, 1024 * zh + 256 * x)):
                    rows = slice(32 * k + 16 * p, 32 * k + 16 * p + 16)
                    v = sf_ref[k * 8 + zh * 4 + x, p].astype(F32)
                    if lanes < 3 * D:
                        gq[rows, lanes : lanes + 256] = v
                    else:
                        ga[rows, lanes - 3 * D : lanes - 3 * D + 256] = v


def per_device(
    tokens, key_mask, image_live, routes, ln1_gain, ln1_bias, w_qkv, w_attn, ln2_gain, ln2_bias,
    w_router, w_in, w_out, cotangent,
):
    images, length, width = tokens.shape
    rows8 = jnp.concatenate(
        [w_router.T, ln1_gain[None], ln1_bias[None], ln2_gain[None], ln2_bias[None], jnp.zeros((8, 64), BF16)], axis=0
    )
    odd = lax.axis_index("fsdp") % 2
    v_in = jnp.concatenate([jnp.where(odd == 0, rows8, 0), jnp.where(odd == 1, rows8, 0)], axis=1)
    bias = jnp.where(key_mask > 0, 0.0, NEG).astype(F32)[:, None, :]
    live = jnp.broadcast_to(image_live.astype(F32)[:, None, None], (images, 1, length))
    prep = jnp.concatenate([routes.transpose(0, 2, 1).astype(F32), bias, live, jnp.zeros((images, 4, length), F32)], axis=1)
    tail = jnp.where(jnp.arange(8) == 2, NEG, 0.0).astype(F32)[None, :, None]
    prep = jnp.concatenate([prep, jnp.broadcast_to(tail, (images, 8, 256 - length))], axis=2)

    sds = jax.ShapeDtypeStruct
    vm = pl.BlockSpec(memory_space=pltpu.VMEM)
    hbm = pl.BlockSpec(memory_space=pl.ANY)
    V = pltpu.VMEM
    S = pltpu.SemaphoreType.DMA
    outs = pl.pallas_call(
        kernel,
        in_specs=[vm, vm, vm, hbm, hbm, hbm, hbm, hbm],
        out_specs=[vm, vm, vm, vm, hbm, hbm, hbm, hbm, hbm],
        out_shape=[
            sds((IMG, LEN, D), BF16),
            sds((IMG, LEN, D), F32),
            sds((16, 2, 16, 256), BF16),
            sds((8, D), F32),
            sds((8, 2 * CH, D), BF16),
            sds((2, 2, 4, 128, CH), BF16),
            sds((4, 2, 4, 2, RA, CH), BF16),
            sds((4, 2, 2, 4, RB, CH), BF16),
            sds((4, 4, 4, RC, CH), BF16),
        ],
        scratch_shapes=[
            V((D, 2048), BF16),
            V((2, 2 * CH, D), BF16),
            V((2, 2, 4, 128, CH), BF16),
            V((ROWS, D), BF16),
            V((D, ROWS), BF16),
            V((ROWS, 3 * D), BF16),
            V((IMG * HEADS, PAD, PAD), BF16),
            V((ROWS, D), BF16),
            V((ROWS, D), F32),
            V((PAIR, D), BF16),
            V((PAIR, D), BF16),
            V((D, PAIR), BF16),
            V((D, PAIR), BF16),
            V((ROWS, 128), F32),
            V((PAIR, 128), BF16),
            V((PAIR, CH), BF16),
            V((PAIR, D), F32),
            V((PAIR, D), F32),
            V((PAIR, CH), F32),
            V((PAIR, 2 * CH), BF16),
            V((ROWS, D), BF16),
            V((ROWS, D), BF16),
            V((ROWS, 128), F32),
            V((ROWS, 128), F32),
            V((8, D), F32),
            V((8, D), F32),
            V((4, 4, 8, D), F32),
            V((ROWS, 128), BF16),
            V((8, 16, 128), BF16),
            V((128, D), BF16),
            V((4, 8, 32, 512), BF16),
            V((4, 2, 4, 32, 512), BF16),
            V((4, 4, 2, 16, 512), BF16),
            V((4, 2, 4, 16, 512), BF16),
            V((4, 2, 16, 512), BF16),
            V((4, 4, 16, 256), BF16),
            V((4, 16, 256), BF16),
            V((4, 16, 256), BF16),
            V((4, 2, 16, 512), BF16),
            V((2, 4, 16, 512), BF16),
            V((2, 16, 512), BF16),
            V((4, 16, 256), BF16),
            V((4, 2, 2, RA, CH), BF16),
            V((4, 4, RB, CH), BF16),
            V((4, 4, RC, CH), BF16),
            V((4, RA, CH), BF16),
            V((4, RB, CH), BF16),
            V((4, RC, CH), BF16),
            S((11,)),
            S((2, 2, 4)),
            S((2, 2, 2, 4)),
            S((2, 2, 2, 4)),
            S((2, 4)),
            S((2, 4)),
            S((2, 8)),
            S((2, 3, 4)),
            S((2, 2, 8)),
            S((2, 12)),
            S((2, 6)),
            S((2, 3)),
            S((3, 4)),
            S((4, 4)),
            S((2, 16, 4)),
            S((2, 4, 4)),
            S((2,)),
            S((2, 16)),
        ],
        compiler_params=pltpu.CompilerParams(
            collective_id=0, has_side_effects=True, vmem_limit_bytes=61 * 1024 * 1024
        ),
        cost_estimate=pl.CostEstimate(flops=50_000_000_000, bytes_accessed=60_000_000, transcendentals=10_000_000),
        name="layer",
    )(tokens, prep, cotangent, w_qkv, w_attn, v_in, w_in, w_out)
    layer_out, grad_tokens, sf, misc, _, f_all = outs[:6]
    g_in, g_out, g_qkv, g_attn = pl.pallas_call(
        finish,
        grid=(4,),
        in_specs=[
            pl.BlockSpec((2, 2, D, 128), lambda e: (0, 0, 0, e)),
            pl.BlockSpec((16, 2, 16, 256), lambda e: (0, 0, 0, 0)),
        ],
        out_specs=[
            pl.BlockSpec((1, D, 256), lambda e: (e, 0, 0)),
            pl.BlockSpec((1, 256, D), lambda e: (e, 0, 0)),
            pl.BlockSpec((64, 3 * D), lambda e: (0, 0)),
            pl.BlockSpec((64, D), lambda e: (0, 0)),
        ],
        out_shape=[sds((4, D, 256), F32), sds((4, 256, D), F32), sds((64, 3 * D), F32), sds((64, D), F32)],
        name="finish",
    )(f_all.reshape(2, 2, D, CH), sf)
    mine = lax.dynamic_slice(misc, (0, 64 * lax.axis_index("fsdp")), (8, 64))
    return (layer_out, grad_tokens, mine[4], mine[5], g_qkv, g_attn, mine[6], mine[7], mine[:4].T, g_in, g_out)


def solution(mesh):
    dev = ("dp", "fsdp", "seq")
    in_specs = (
        P(dev, None, None), P(dev, None), P(dev), P(dev, None, None), P("fsdp"), P("fsdp"), P("fsdp", None),
        P("fsdp", None), P("fsdp"), P("fsdp"), P("fsdp", None), P(None, None, "fsdp"), P(None, "fsdp", None),
        P(dev, None, None),
    )
    out_specs = (
        P(dev, None, None), P(dev, None, None), P("fsdp"), P("fsdp"), P("fsdp", None), P("fsdp", None), P("fsdp"),
        P("fsdp"), P("fsdp", None), P(None, None, "fsdp"), P(None, "fsdp", None),
    )
    return jax.shard_map(per_device, mesh=mesh, in_specs=in_specs, out_specs=out_specs, check_vma=False)
```

```python
import jax
import jax.numpy as jnp
from jax import lax
from jax.experimental import pallas as pl
from jax.experimental.pallas import tpu as pltpu
from jax.sharding import PartitionSpec as P

F32 = jnp.float32
BF16 = jnp.bfloat16
MESH = pl.DeviceIdType.MESH
HEADS = 8
EPS = 1e-06
NEG = -1000000000.0
D = 512
IMG = 4
LEN = 200
PAD = 208
ROWS = IMG * PAD
PAIR = 2 * ROWS
HD = 64
CH = 512
TM = 832
RA, RB, RC = 48, 48, 32


def dot(a, b):
    return jnp.dot(a, b, preferred_element_type=F32)


def dot_nt(a, b):
    return lax.dot_general(a, b, (((1,), (1,)), ((), ())), preferred_element_type=F32)


def dot_tn(a, b):
    return lax.dot_general(a, b, (((0,), (0,)), ((), ())), preferred_element_type=F32)


def rows_of(i):
    return pl.ds(pl.multiple_of(i * PAD, 16), PAD)


def span(start, size, unit):
    return pl.ds(pl.multiple_of(start, unit), size)


def pad_rows(v):
    return jnp.concatenate([v, jnp.zeros((PAD - LEN, v.shape[1]), v.dtype)], axis=0)


def normalize(v):
    c = v - jnp.mean(v, axis=-1, keepdims=True)
    r = lax.rsqrt(jnp.mean(c * c, axis=-1, keepdims=True) + EPS)
    return c * r, r


def lane(shape):
    return lax.broadcasted_iota(jnp.int32, shape, 1)


def loop(lo, hi, body):
    def step(i, carry):
        body(i)
        return carry

    lax.fori_loop(lo, hi, step, 0)


def norm_back(u, n, r):
    return r * (u - jnp.mean(u, axis=-1, keepdims=True) - n * jnp.mean(u * n, axis=-1, keepdims=True))


def ln_one(tok, mt, h1):
    def body(i):
        n, _ = normalize(pad_rows(tok[i].astype(F32)))
        h1[rows_of(i)] = (n * mt[4:5] + mt[5:6]).astype(BF16)

    loop(0, IMG, body)


def make_qkv(s_ref, h1, qkv):
    for b in range(3):
        v = dot(h1[...], s_ref[:, D * b : D * b + D]).astype(BF16)
        if b == 0:
            v = v * jnp.asarray(HD**-0.5, BF16)
        qkv[:, D * b : D * b + D] = v


def attend(i, qkv, prep, pb, ob):
    r = rows_of(i)
    bias = prep[i, 2:3, :PAD]
    low = lane((PAD, 128)) < HD
    for hp in range(HEADS // 2):
        o = 128 * hp
        q2, k2, v2 = qkv[r, o : o + 128], qkv[r, D + o : D + o + 128], qkv[r, 2 * D + o : 2 * D + o + 128]
        outs = []
        for a in range(2):
            qm = jnp.where(low if a == 0 else ~low, q2, jnp.zeros_like(q2))
            s = dot_nt(qm, k2) + bias
            e = jnp.exp(s - jnp.max(s, axis=-1, keepdims=True))
            p = (e * (1.0 / jnp.sum(e, axis=-1, keepdims=True))).astype(BF16)
            pb[i * HEADS + hp * 2 + a] = p
            outs.append(dot(p, v2))
        ob[r, o : o + 128] = jnp.where(low, outs[0], outs[1]).astype(BF16)


def middle(i, tok, s_ref, mt, mtb, ob, aux, x1, h2, gates, comb):
    r = rows_of(i)
    v = pad_rows(tok[i].astype(F32)) + dot(ob[r], s_ref[:, 3 * D :])
    x1[r] = v
    n, _ = normalize(v)
    h = (n * mt[6:7] + mt[7:8]).astype(BF16)
    h2[r] = h
    lg = dot_nt(h, mtb[...])
    ok = lane((PAD, 128)) < 4
    lg = jnp.where(ok, lg, -1e30)
    e = jnp.exp(lg - jnp.max(lg, axis=-1, keepdims=True))
    g = e / jnp.sum(e, axis=-1, keepdims=True)
    gates[r] = g
    comb[r] = jnp.where(ok, g * aux[r].astype(F32), 0.0).astype(BF16)


def masks(i, prep, aux):
    row = lax.broadcasted_iota(jnp.int32, (128, 256), 0)
    v = prep[i]
    e = row.astype(F32)
    hit = ((v[0:1] == e) | (v[1:2] == e)) & (row < 4)
    flags = jnp.where(hit, 1.0, jnp.where(row == 4, v[3:4], 0.0))
    aux[rows_of(i)] = jnp.transpose(flags)[:PAD].astype(BF16)


def live_cotangent(i, cot, aux, gm):
    r = rows_of(i)
    gm[r] = (pad_rows(cot[i].astype(F32)) * aux[r, 4:5].astype(F32)).astype(BF16)


def expander():
    return (
        lax.broadcasted_iota(jnp.int32, (128, CH), 0) == lax.broadcasted_iota(jnp.int32, (128, CH), 1) // 128
    ).astype(BF16)


def experts_tile(lo, w, h2, gm, cx, gca, m, gh2, cag):
    r = pl.ds(lo, TM)
    win, wout = w[:CH], w[CH:]
    hid = dot(h2[r], win)
    ga = dot_nt(gm[r], wout)
    cdf = 0.5 * (1.0 + lax.erf(hid * 0.7071067811865476))
    slope = cdf + hid * jnp.exp(-0.5 * hid * hid) * 0.3989422804014327
    act = hid * cdf
    c = cx[r].astype(F32)
    gca[r] += act * ga
    ca = (act * c).astype(BF16)
    gh = (ga * c * slope).astype(BF16)
    cag[r, :CH] = ca
    cag[r, CH:] = gh
    m[r] += dot(ca, wout)
    gh2[r] += dot_nt(gh, win)


def layer_result(i, tok, aux, m, mr, out):
    r = rows_of(i)
    v = m[r] + mr[r].astype(F32)
    out[i] = jnp.where(aux[r, 4:5].astype(F32) > 0, v, pad_rows(tok[i].astype(F32)))[:LEN].astype(BF16)


def second_norm_back(i, mtb, mt, aux, gates, gca, gcr, gh2, gh2r, gm, x1, m, glb, gab, vec):
    r = rows_of(i)
    ok = lane((PAD, 128)) < 4
    ch = jnp.where(ok, aux[r].astype(F32), 0.0)
    g = gates[r]
    gg = (dot_nt(gca[r].astype(BF16), expander()) + gcr[r]) * ch
    gl = (g * (gg - jnp.sum(gg * g, axis=-1, keepdims=True))).astype(BF16)
    glb[r] = gl
    gh = gh2[r] + gh2r[r].astype(F32) + dot(gl, mtb[...])
    n, r2 = normalize(x1[r])
    vec[6:7] += jnp.sum(gh * n, axis=0, keepdims=True)
    vec[7:8] += jnp.sum(gh, axis=0, keepdims=True)
    gx = gm[r].astype(F32) + norm_back(gh * mt[6:7], n, r2)
    m[r] += x1[r]
    x1[r] = gx
    gab[r] = gx.astype(BF16)


def attend_back(i, qkv, pb, cag):
    r = rows_of(i)
    rv = span(ROWS + i * PAD, PAD, 16)
    low = lane((PAD, 128)) < HD
    for hp in range(HEADS // 2):
        o = 128 * hp
        q2, k2, v2 = qkv[r, o : o + 128], qkv[r, D + o : D + o + 128], qkv[r, 2 * D + o : 2 * D + o + 128]
        g2 = cag[rv, D + o : D + o + 128]
        gq, gk, gv = [], [], []
        for a in range(2):
            gmk = jnp.where(low if a == 0 else ~low, g2, jnp.zeros_like(g2))
            p = pb[i * HEADS + hp * 2 + a]
            pf = p.astype(F32)
            t = dot_nt(gmk, v2)
            gs = (pf * (t - jnp.sum(t * pf, axis=-1, keepdims=True))).astype(BF16)
            gq.append(dot(gs, k2))
            gk.append(dot_tn(gs, q2))
            gv.append(dot_tn(p, g2))
        cag[r, o : o + 128] = (jnp.where(low, gq[0], gq[1]) * HD**-0.5).astype(BF16)
        cag[r, D + o : D + o + 128] = jnp.where(low, gk[0], gk[1]).astype(BF16)
        cag[rv, o : o + 128] = jnp.where(low, gv[0], gv[1]).astype(BF16)


def first_norm_back(i, tok, cot, aux, s_ref, mt, cag, x1, vec, gt):
    r = rows_of(i)
    rv = span(ROWS + i * PAD, PAD, 16)
    gh = (
        dot_nt(cag[r, :D], s_ref[:, :D])
        + dot_nt(cag[r, D:], s_ref[:, D : 2 * D])
        + dot_nt(cag[rv, :D], s_ref[:, 2 * D : 3 * D])
    )
    n, r1 = normalize(pad_rows(tok[i].astype(F32)))
    vec[4:5] += jnp.sum(gh * n, axis=0, keepdims=True)
    vec[5:6] += jnp.sum(gh, axis=0, keepdims=True)
    gd = jnp.where(aux[r, 4:5].astype(F32) > 0, 0.0, pad_rows(cot[i].astype(F32)))
    gt[i] = (gd + x1[r] + norm_back(gh * mt[4:5], n, r1))[:LEN]


def order(k):
    dy = jnp.where((k == 1) | (k == 4), 2, jnp.where((k == 2) | (k == 5), 1, jnp.where((k == 3) | (k == 6), 3, 0)))
    dz = jnp.where(k >= 4, 1, 0)
    return dz, dy


def kernel(
    tok, prep, cot, q_in, a_in, v_in, w_in, w_out,
    out, gt, sf, misc, w_all, f_all, r1a, r1b, r1c,
    s_ref, wbuf, gst, h1, h1t, qkv, pb, ob, x1, h2, gm, h2t, gmt, gates, comb, cx, m, gh2, gca, cag,
    gh2r, mr, gcp, gcr, mt, vec, mx, aux, mtg, mtb,
    cr, gc, qa1, qb1, qa2, qb2, qa3, qb3, ga2, gb2, ga3, gb3, r2a, r2b, r2c,
    r3a, r3b, r3c,
    lsem, sy, sz, sc, vy, vz, wy, wx, wz, px, ssem, lsem2, rsem, asem, gsem, msem, wsem, bsem,
):
    zh, f, sq = lax.axis_index("dp"), lax.axis_index("fsdp"), lax.axis_index("seq")
    zl, y = f // 4, f % 4
    x, c = sq // 2, sq % 2
    z = zh * 2 + zl

    def dev(zh_=zh, zl_=zl, y_=y, x_=x, c_=c):
        return (zh_, zl_ * 4 + y_, x_ * 2 + c_)

    def up(v, d):
        return (v + d) % 4

    def dev_z(zz):
        return dev(zh_=zz // 2, zl_=zz % 2)

    core = dev(c_=1 - c)

    def rdma(src, dst, ssm, rsm, target):
        return pltpu.make_async_remote_copy(
            src_ref=src, dst_ref=dst, send_sem=ssm, recv_sem=rsm, device_id=target, device_id_type=MESH
        )

    barrier = pltpu.get_barrier_semaphore()
    for d in (1, 2, 3):
        for target in (dev(x_=up(x, d)), dev(y_=up(y, d)), dev_z(up(z, d))):
            pl.semaphore_signal(barrier, inc=1, device_id=target, device_id_type=MESH)
    others = [(1, 0, 0)] + [(dc, dzh, d) for dc in (0, 1) for dzh in (0, 1) for d in range(4) if d and dc + dzh]
    others += [(1, 1, 0)]
    for dc, dzh, d in others:
        target = dev(c_=(c + dc) % 2, zh_=(zh + dzh) % 2, x_=up(x, d))
        pl.semaphore_signal(barrier, inc=1, device_id=target, device_id_type=MESH)

    own = [
        pltpu.make_async_copy(q_in, s_ref.at[span(64 * f, 64, 64), : 3 * D], lsem.at[0]),
        pltpu.make_async_copy(a_in, s_ref.at[span(64 * f, 64, 64), 3 * D :], lsem.at[9]),
        pltpu.make_async_copy(v_in, mtg.at[f], lsem.at[10]),
    ]
    half = span(128 * c, 128, 128)
    for e in range(4):
        own.append(
            pltpu.make_async_copy(w_in.at[e, :, half], wbuf.at[0, :CH, 128 * e : 128 * e + 128], lsem.at[1 + e])
        )
        own.append(
            pltpu.make_async_copy(w_out.at[e, half, :], wbuf.at[0, CH + 128 * e : CH + 128 * e + 128], lsem.at[5 + e])
        )
    for cp in own:
        cp.start()
    pl.semaphore_wait(barrier, 9 + len(others))
    for cp in own[:3]:
        cp.wait()

    cols = (slice(0, 3 * D), slice(3 * D, 4 * D))

    def s_part(p, zz, yy, cc, size=32, off=0):
        return s_ref.at[span((zz * 4 + yy) * 64 + 32 * cc + off, size, 16), cols[p]]

    def s_y(p, d):
        r = s_part(p, zl, y, c)
        return rdma(r, r, sy.at[0, p, d], sy.at[1, p, d], dev(y_=up(y, d)))

    def s_z(p, way, d):
        r = s_part(p, zl, up(y, 4 - d), c, 16, 16 * way)
        return rdma(r, r, sz.at[0, p, way, d], sz.at[1, p, way, d], dev_z(up(z, 1 if way == 0 else 3)))

    def s_c(p, dz, d):
        r = s_part(p, (zl + dz) % 2, up(y, 4 - d), c)
        return rdma(r, r, sc.at[0, p, dz, d], sc.at[1, p, dz, d], core)

    def v_y(d):
        return rdma(mtg.at[f], mtg.at[f], vy.at[0, d], vy.at[1, d], dev(y_=up(y, d)))

    def v_z(d):
        r = mtg.at[zl * 4 + up(y, 4 - d)]
        return rdma(r, r, vz.at[0, d], vz.at[1, d], dev_z(up(z, 1)))

    def s_z_done(p):
        for d in (0, 1, 3, 2):
            for way in (0, 1):
                s_z(p, way, d).wait_recv()
            s_c(p, 1, d).start()

    def s_c_done(p):
        for dz in (0, 1):
            for d in range(4):
                if (dz, d) != (0, 0):
                    s_c(p, dz, d).wait_recv()

    for d in (1, 3, 2):
        v_y(d).start()
    v_z(0).start()
    for d in (1, 3, 2):
        s_y(0, d).start()
    for way in (0, 1):
        s_z(0, way, 0).start()

    loop(0, IMG, lambda i: (masks(i, prep, aux), live_cotangent(i, cot, aux, gm)))
    own_rows, peer_rows = pl.ds(0, ROWS), pl.ds(ROWS, ROWS)
    gm_x = rdma(gm.at[own_rows], gm.at[peer_rows], px.at[0, 0], px.at[1, 0], core)

    for d in (1, 3, 2):
        v_y(d).wait_recv()
        v_z(d).start()
    def s_y_done(p):
        for d in (1, 3, 2):
            s_y(p, d).wait_recv()
            for way in (0, 1):
                s_z(p, way, d).start()
            s_c(p, 0, d).start()

    s_y_done(0)
    for d in (1, 3, 2):
        s_y(1, d).start()

    def w_y(d, h=0):
        r = w_all.at[f, span(256 * x, 256, 256)] if d == 2 else w_all.at[f, CH * h : CH * h + CH]
        return rdma(r, r, wy.at[0, d + 4 * h], wy.at[1, d + 4 * h], dev(y_=up(y, d)))

    def w_x(n, d):
        dz, dy = ((0, 2), (1, 0), (1, 2))[n]
        r = w_all.at[((zl + dz) % 2) * 4 + up(y, dy), span(256 * x, 256, 256)]
        return rdma(r, r, wx.at[0, n, d], wx.at[1, n, d], dev(x_=up(x, d)))

    def w_z(way, d, h=0):
        chunk_of = w_all.at[zl * 4 + up(y, 4 - d)]
        if d % 2 == 0:
            r = chunk_of.at[span(256 * x + 128 * way, 128, 128)]
        else:
            r = chunk_of.at[CH * h + 256 * way : CH * h + 256 * way + 256]
        return rdma(r, r, wz.at[0, way, d + 4 * h], wz.at[1, way, d + 4 * h], dev_z(up(z, 1 if way == 0 else 3)))

    all_w_y = [(2, 0), (1, 0), (3, 0), (1, 1), (3, 1)]
    all_w_z = [(way, d, h) for d, h in [(0, 0), (2, 0), (1, 0), (3, 0), (1, 1), (3, 1)] for way in (0, 1)]

    for cp in own[3:]:
        cp.wait()
    w_own = pltpu.make_async_copy(wbuf.at[0], w_all.at[f], lsem.at[0])
    w_own.start()
    w_own.wait()
    for d, h in all_w_y[:3]:
        w_y(d, h).start()

    gm_x.start()
    gmt[:, :ROWS] = gm[:ROWS].T
    for d in range(4):
        v_z(d).wait_recv()
    mt[...] = jnp.concatenate([(mtg[2 * i, :8] + mtg[2 * i + 1, :8]).astype(F32) for i in range(4)], axis=1)
    mtb[...] = jnp.concatenate([mt[...], jnp.zeros((120, D), F32)], axis=0).astype(BF16)
    vec[...] = jnp.zeros_like(vec)
    ln_one(tok, mt, h1)
    s_z_done(0)
    for way in (0, 1):
        s_z(1, way, 0).start()
    s_y_done(1)
    for way in (0, 1):
        w_z(way, 0).start()
    m[...] = jnp.zeros_like(m)
    gh2[...] = jnp.zeros_like(gh2)
    gca[...] = jnp.zeros_like(gca)
    h1t[...] = h1[...].T
    gm_x.wait_recv()
    gmt[:, ROWS:] = gm[ROWS:].T
    s_c_done(0)

    make_qkv(s_ref, h1, qkv)
    s_z_done(1)
    w_y(2).wait_recv()
    for d in (1, 2, 3):
        w_x(0, d).start()
    for way in (0, 1):
        w_z(way, 2).start()
    s_c_done(1)

    def h2_x(i):
        return rdma(h2.at[rows_of(i)], h2.at[span(ROWS + i * PAD, PAD, 16)], px.at[0, 3 + i], px.at[1, 3 + i], core)

    def comb_x(i):
        return rdma(comb.at[rows_of(i)], comb.at[span(ROWS + i * PAD, PAD, 16)], px.at[0, 7 + i], px.at[1, 7 + i], core)

    def forward(i):
        attend(i, qkv, prep, pb, ob)
        middle(i, tok, s_ref, mt, mtb, ob, aux, x1, h2, gates, comb)
        h2_x(i).start()
        comb_x(i).start()

    loop(0, 2, forward)
    for d in (1, 3):
        w_y(d, 0).wait_recv()
        w_y(d, 1).start()
        for way in (0, 1):
            w_z(way, d, 0).start()
    loop(2, IMG, forward)
    for way in (0, 1):
        w_z(way, 2).wait_recv()
    for d in (1, 2, 3):
        w_x(2, d).start()
    h2t[:, :ROWS] = h2[:ROWS].T

    def load_w(k):
        dz, dy = order(k)
        return pltpu.make_async_copy(w_all.at[((zl + dz) % 2) * 4 + up(y, 4 - dy)], wbuf.at[k % 2], wsem.at[k % 2])

    ex = expander()
    cx[:ROWS] = dot(comb[:ROWS], ex).astype(BF16)
    loop(0, IMG, lambda i: (h2_x(i).wait_recv(), comb_x(i).wait_recv()))
    h2t[:, ROWS:] = h2[ROWS:].T
    cx[ROWS:] = dot(comb[ROWS:], ex).astype(BF16)

    def sends(k, act):
        slot = k % 2
        dz, dy = order(k)
        zz, yy = (zl + dz) % 2, up(y, 4 - dy)

        def local(src, dst, i):
            cp = pltpu.make_async_copy(src, dst, lsem2.at[slot, i])
            cp.start() if act == 0 else cp.wait()

        def remote(src, dst, i, rsm, target):
            cp = rdma(src, dst, ssem.at[slot, i], rsm, target)
            cp.start() if act == 0 else cp.wait_send()

        g = gst.at[slot]
        for d in (1, 2, 3):
            remote(g.at[:, up(x, d), :RA], r1a.at[d, zz, yy], d - 1, rsem.at[0, d], dev(x_=up(x, d)))
        local(g.at[:, x, :RA], r1a.at[0, zz, yy], 0)

        @pl.when(dy != 0)
        def _():
            remote(g.at[:, :, RA : RA + RB], r1b.at[dy, zz], 3, rsem.at[1, dy], dev(y_=yy))

        @pl.when(dy == 0)
        def _():
            local(g.at[:, :, RA : RA + RB], r1b.at[0, zz], 1)

        remote(g.at[1 - zh, :, RA + RB :], r1c.at[2 + dz, yy], 4, rsem.at[2, 2 + dz], dev(zh_=1 - zh, zl_=zz))

        @pl.when(dz != 0)
        def _():
            remote(g.at[zh, :, RA + RB :], r1c.at[1, yy], 5, rsem.at[2, 1], dev(zl_=zz))

        @pl.when(dz == 0)
        def _():
            local(g.at[zh, :, RA + RB :], r1c.at[0, yy], 2)

    gh2_x = rdma(cx.at[peer_rows], gh2r, px.at[0, 1], px.at[1, 1], core)
    gcp_x = rdma(gcp, gcr, px.at[0, 2], px.at[1, 2], core)
    m_x = rdma(h1, mr, px.at[0, 11], px.at[1, 11], core)

    def chunk(k):
        slot = k % 2
        w = wbuf.at[slot]
        experts_tile(ROWS, w, h2, gm, cx, gca, m, gh2, cag)

        @pl.when(k < 7)
        def _():
            nxt = k + 1

            for n, part in ((1, 0), (4, 2), (7, 1)):

                @pl.when(nxt == n)
                def _(part=part):
                    for d in (1, 2, 3):
                        w_x(part, d).wait_recv()

            @pl.when(nxt == 2)
            def _():
                for d in (1, 3):
                    w_y(d, 1).wait_recv()
                    for way in (0, 1):
                        w_z(way, d, 1).start()
                for way in (0, 1):
                    w_z(way, 0).wait_recv()
                for d in (1, 2, 3):
                    w_x(1, d).start()

            for n, d in ((5, 1), (6, 3)):

                @pl.when(nxt == n)
                def _(d=d):
                    for h in (0, 1):
                        for way in (0, 1):
                            w_z(way, d, h).wait_recv()

            load_w(nxt).start()

        @pl.when(k == 7)
        def _():
            cx[ROWS:] = gh2[ROWS:].astype(BF16)
            gh2_x.start()
            gcp[...] = dot_nt(gca[ROWS:].astype(BF16), expander())
            gcp_x.start()
            h1[...] = m[ROWS:].astype(BF16)
            m_x.start()

        experts_tile(0, w, h2, gm, cx, gca, m, gh2, cag)

        @pl.when(k >= 2)
        def _():
            sends(k - 2, 1)

        for b in range(2):
            gv = dot((h2t if b == 0 else gmt)[...], cag[:, (CH if b == 0 else 0) : (2 * CH if b == 0 else CH)])
            gst[slot, b] = gv.astype(BF16).reshape(4, 128, CH)
        sends(k, 0)

        @pl.when(k < 7)
        def _():
            load_w(k + 1).wait()

    loop(0, 8, chunk)

    glb, gab = comb.at[peer_rows], gm.at[peer_rows]
    flat = wbuf.reshape(4 * CH, D)
    p1a = flat.at[: 16 * RA].reshape(2, 4, 2, RA, CH)
    p1b = flat.at[16 * RA : 16 * (RA + RB)].reshape(2, 2, 4, RB, CH)
    p1c = flat.at[16 * (RA + RB) :].reshape(4, 4, RC, CH)
    gs = gst.reshape(4, 8, 64, D)
    p2a = ob.at[: 4 * RA].reshape(2, 2, RA, CH)
    p2b = ob.at[4 * RA : 4 * (RA + RB)].reshape(4, RB, CH)
    p2c = ob.at[4 * (RA + RB) : 512].reshape(4, RC, CH)
    fp = ob.at[512:640]

    gh2_x.wait_recv()
    gcp_x.wait_recv()
    def second(i):
        second_norm_back(i, mtb, mt, aux, gates, gca, gcr, gh2, gh2r, gm, x1, m, glb, gab, vec)

    loop(0, IMG, second)
    cag[ROWS:, D:] = dot_nt(gab[...], s_ref[:, 3 * D :]).astype(BF16)
    loop(0, 1, lambda i: attend_back(i, qkv, pb, cag))

    started = []

    def go(copies):
        for cp in copies:
            cp.start()
        started.extend(copies)
        return copies

    def arrived(copies):
        for cp in copies:
            cp.wait_recv()

    def by_x(src, dst, n):
        return [
            rdma(src(up(x, d)), dst(d), gsem.at[0, n, d], gsem.at[1, n, d], dev(x_=up(x, d))) for d in (1, 2, 3)
        ]

    def by_y(src, dst, n):
        return [
            rdma(src(up(y, d)), dst(d), gsem.at[0, n, d], gsem.at[1, n, d], dev(y_=up(y, d))) for d in (1, 2, 3)
        ]

    def by_z(src, dst, n):
        copies = []
        for q in (1, 2, 3):
            zhv, zlv = (zh + q // 2) % 2, (zl + q % 2) % 2
            copies.append(rdma(src(zlv, zhv), dst(q), gsem.at[0, n, q], gsem.at[1, n, q], dev(zh_=zhv, zl_=zlv)))
        return copies

    def total(first, rest):
        acc = first.astype(F32)
        for d in (1, 2, 3):
            acc = acc + rest[d].astype(F32)
        return acc.astype(BF16)

    sends(6, 1)
    sends(7, 1)
    def part_in(part, recv):
        for d in (1, 2, 3):
            rdma(recv.at[d], recv.at[d], ssem.at[0, 0], rsem.at[part, d], core).wait_recv()

    part_in(0, r1a)

    gh2_x.wait_send()
    room = 16 * RA
    bufs = [gst.reshape(2, 2 * CH, CH).at[i, :room] for i in range(2)] + [cx.at[i * room : i * room + room] for i in range(2)]
    pieces = [((4, 2, 2, RA, CH), lambda s, i=i: r1a.at[s, i // 2, 2 * (i % 2) : 2 * (i % 2) + 2]) for i in range(4)]
    pieces += [((4, 4, RB, CH), lambda s, i=i: r1b.at[s, i // 2, i % 2]) for i in range(4)]
    pieces += [((4, 4, RC, CH), lambda s, i=i: r1c.at[s, i]) for i in range(4)]

    def piece(n):
        shape, src = pieces[n]
        rows = 16 * shape[-2] if len(shape) == 4 else room
        v = bufs[n % 4].at[:rows].reshape(*shape)
        return v, [pltpu.make_async_copy(src(s), v.at[s], asem.at[n % 4, s]) for s in range(4)]

    for n in range(4):
        for cp in piece(n)[1]:
            cp.start()
    for n in range(12):
        v, copies = piece(n)
        for cp in copies:
            cp.wait()
        t = total(v[0], v)
        if n < 4:
            p1a[n // 2, 2 * (n % 2) : 2 * (n % 2) + 2] = t
        elif n < 8:
            p1b[(n - 4) // 2, (n - 4) % 2] = t
        else:
            p1c[n - 8] = t
        if n == 0:
            part_in(1, r1b)
        if n == 4:
            part_in(2, r1c)
        if n + 4 < 12:
            for cp in piece(n + 4)[1]:
                cp.start()
        if n == 3:
            s2a = go(by_y(lambda v: p1a.at[:, v], lambda d: r2a.at[d], 0))
        if n == 7:
            s2b = go(by_z(lambda zlv, zhv: p1b.at[zlv, zhv], lambda d: r2b.at[d], 1))
    s2c = go(by_x(lambda v: p1c.at[:, v], lambda d: r2c.at[d], 2))

    def core_go(b, gv):
        gs[b] = gv.astype(BF16).reshape(8, 64, D)
        return go([rdma(gs.at[b, :, span(32 * (1 - c), 32, 32)], cr.at[b], gsem.at[0, 3, b], gsem.at[1, 3, b], core)])

    s_core = core_go(3, dot_tn(ob[...], gab[...]))
    loop(1, 3, lambda i: attend_back(i, qkv, pb, cag))

    arrived(s2a)
    p2a[...] = total(p1a[:, y], r2a)
    s3a = go(by_z(lambda zlv, zhv: p2a.at[zlv, zhv], lambda d: r3a.at[d], 4))
    arrived(s2b)
    p2b[...] = total(p1b[zl, zh], r2b)
    s3b = go(by_x(lambda v: p2b.at[v], lambda d: r3b.at[d], 5))
    arrived(s2c)
    p2c[...] = total(p1c[:, x], r2c)
    s3c = go(by_y(lambda v: p2c.at[v], lambda d: r3c.at[d], 6))

    loop(3, 4, lambda i: attend_back(i, qkv, pb, cag))

    for b in range(3):
        s_core += core_go(b, dot(h1t[...], cag[:ROWS, D * b : D * b + D] if b < 2 else cag[ROWS:, :D]))

    arrived(s3a)
    fp[:RA] = total(p2a[zl, zh], r3a)
    arrived(s3b)
    fp[RA : RA + RB] = total(p2b[x], r3b)
    arrived(s3c)
    fp[RA + RB :] = total(p2c[y], r3c)
    fl, fr = slice(0, 256), slice(256, 512)
    f_own = pltpu.make_async_copy(fp, f_all.at[c, zh, x], lsem.at[0])
    f_own.start()
    across = dev(zh_=1 - zh)
    f_1l = go([rdma(fp.at[:, fl], f_all.at[c, zh, x, :, fl], gsem.at[0, 9, 1], gsem.at[1, 9, 1], across)])
    f_1r = go(by_x(lambda v: fp.at[:, fr], lambda d: f_all.at[c, zh, x, :, fr], 15))

    arrived(s_core)

    def core_sum(j):
        mine = gs[:, j, span(32 * c, 32, 32)]
        gc[:, j // 4, j % 4] = (mine.astype(F32) + cr[:, j].astype(F32)).astype(BF16)

    loop(0, 8, core_sum)
    t1a = go(by_y(lambda v: gc.at[:, :, v, 0:16], lambda d: qa1.at[d], 7))
    t1b = go(by_z(lambda zlv, zhv: gc.at[span(2 * zhv, 2, 2), zlv, :, 16:32], lambda d: qb1.at[d], 8))

    last = lambda i: first_norm_back(i, tok, cot, aux, s_ref, mt, cag, x1, vec, gt)
    loop(0, 2, last)
    f_own.wait()
    arrived(f_1l)
    f_2l = go(by_x(lambda v: f_all.at[c, :, x, :, fl], lambda d: f_all.at[c, :, x, :, fl], 12))
    arrived(f_1r)
    r_part = f_all.at[c, zh, :, :, fr]
    f_2r = go([rdma(r_part, r_part, gsem.at[0, 9, 2], gsem.at[1, 9, 2], across)])
    loop(2, IMG, last)

    mr_g = dot_tn(glb[...], h2[:ROWS])
    row = lax.broadcasted_iota(jnp.int32, (8, D), 0)
    mx[0, c] = jnp.where(row < 4, mr_g[:8], vec[...])

    def misc_go(n, me, targets):
        return go([rdma(mx.at[n, me], mx.at[n, me], msem.at[0, n, d], msem.at[1, n, d], t) for d, t in targets])

    def misc_sum(n, count):
        acc = mx[n, 0]
        for i in range(1, count):
            acc = acc + mx[n, i]
        return acc

    m0 = misc_go(0, c, [(1, core)])

    arrived(t1a)
    ga2[...] = total(gc[:, :, y, 0:16], qa1)
    t2a = go(by_x(lambda v: ga2.at[v], lambda d: qa2.at[d], 10))
    arrived(t1b)
    gb2[...] = total(gc[span(2 * zh, 2, 2), zl, :, 16:32], qb1)
    t2b = go(by_x(lambda v: gb2.at[v // 2, :, :, span(256 * (v % 2), 256, 256)], lambda d: qb2.at[d], 11))

    m_x.wait_recv()
    loop(0, IMG, lambda i: layer_result(i, tok, aux, m, mr, out))

    arrived(m0)
    mx[1, x] = misc_sum(0, 2)
    m1 = misc_go(1, x, [(d, dev(x_=up(x, d))) for d in (1, 2, 3)])

    arrived(t2a)
    ga3[...] = total(ga2[x], qa2)
    t3a = go(by_z(lambda zlv, zhv: ga3.at[zlv, :, span(256 * zhv, 256, 256)], lambda d: qa3.at[d], 13))
    arrived(t2b)
    gb3[...] = total(gb2[x // 2, :, :, span(256 * (x % 2), 256, 256)], qb2)
    t3b = go(by_y(lambda v: gb3.at[v], lambda d: qb3.at[d], 14))

    arrived(m1)
    mx[2, y] = misc_sum(1, 4)
    m2 = misc_go(2, y, [(d, dev(y_=up(y, d))) for d in (1, 2, 3)])

    me = c * 8 + zh * 4 + x
    arrived(t3a)
    sf[me, 0] = total(ga3[zl, :, span(256 * zh, 256, 256)], qa3)
    arrived(t3b)
    sf[me, 1] = total(gb3[y], qb3)
    t4 = []
    for d in range(1, 16):
        target = dev(c_=(c + d // 8) % 2, zh_=(zh + d // 4) % 2, x_=up(x, d % 4))
        t4.append(rdma(sf.at[me], sf.at[me], bsem.at[0, d], bsem.at[1, d], target))
    go(t4)

    arrived(m2)
    mx[3, z] = misc_sum(2, 4)
    m3 = misc_go(3, z, [(d, dev_z(up(z, d))) for d in (1, 2, 3)])
    arrived(f_2l)
    arrived(f_2r)
    f_c = go([rdma(f_all.at[c], f_all.at[c], gsem.at[0, 9, 3], gsem.at[1, 9, 3], core)])
    arrived(m3)
    misc[...] = misc_sum(3, 4)
    arrived(t4)
    arrived(f_c)

    for cp in started:
        cp.wait_send()
    for cp in [gm_x, gcp_x, m_x]:
        cp.wait_send()
    loop(0, IMG, lambda i: (h2_x(i).wait_send(), comb_x(i).wait_send()))
    for d in (1, 2, 3):
        v_y(d).wait_send()
        for n in range(3):
            w_x(n, d).wait_send()
    for d, h in all_w_y:
        w_y(d, h).wait_send()
    for way, d, h in all_w_z:
        w_z(way, d, h).wait_send()
    for d in range(4):
        v_z(d).wait_send()
        for p in (0, 1):
            if d:
                s_y(p, d).wait_send()
            for way in (0, 1):
                s_z(p, way, d).wait_send()
            for dz in (0, 1):
                if (dz, d) != (0, 0):
                    s_c(p, dz, d).wait_send()


def finish(f_ref, sf_ref, o_ref, t_ref, gin, gout, gq, ga, out, gt):
    out[...] = o_ref[...]
    gt[...] = t_ref[...]
    for k in range(2):
        w = slice(128 * k, 128 * k + 128)
        gin[0, :, w] = f_ref[k, 0].astype(F32)
        gout[0, w, :] = jnp.transpose(f_ref[k, 1].astype(F32))
    for k in range(2):
        for zh in range(2):
            for x in range(4):
                for p, lanes in ((0, 512 * x + 256 * zh), (1, 1024 * zh + 256 * x)):
                    rows = slice(32 * k + 16 * p, 32 * k + 16 * p + 16)
                    v = sf_ref[k * 8 + zh * 4 + x, p].astype(F32)
                    if lanes < 3 * D:
                        gq[rows, lanes : lanes + 256] = v
                    else:
                        ga[rows, lanes - 3 * D : lanes - 3 * D + 256] = v


def per_device(
    tokens, key_mask, image_live, routes, ln1_gain, ln1_bias, w_qkv, w_attn, ln2_gain, ln2_bias,
    w_router, w_in, w_out, cotangent,
):
    images, length, width = tokens.shape
    rows8 = jnp.concatenate(
        [w_router.T, ln1_gain[None], ln1_bias[None], ln2_gain[None], ln2_bias[None], jnp.zeros((8, 64), BF16)], axis=0
    )
    odd = lax.axis_index("fsdp") % 2
    v_in = jnp.concatenate([jnp.where(odd == 0, rows8, 0), jnp.where(odd == 1, rows8, 0)], axis=1)
    bias = jnp.where(key_mask > 0, 0.0, NEG).astype(F32)[:, None, :]
    live = jnp.broadcast_to(image_live.astype(F32)[:, None, None], (images, 1, length))
    prep = jnp.concatenate([routes.transpose(0, 2, 1).astype(F32), bias, live, jnp.zeros((images, 4, length), F32)], axis=1)
    tail = jnp.where(jnp.arange(8) == 2, NEG, 0.0).astype(F32)[None, :, None]
    prep = jnp.concatenate([prep, jnp.broadcast_to(tail, (images, 8, 256 - length))], axis=2)

    sds = jax.ShapeDtypeStruct
    vm = pl.BlockSpec(memory_space=pltpu.VMEM)
    hbm = pl.BlockSpec(memory_space=pl.ANY)
    V = pltpu.VMEM
    S = pltpu.SemaphoreType.DMA
    outs = pl.pallas_call(
        kernel,
        in_specs=[vm, vm, vm, hbm, hbm, hbm, hbm, hbm],
        out_specs=[vm, vm, vm, vm, hbm, hbm, hbm, hbm, hbm],
        out_shape=[
            sds((IMG, LEN, D), BF16),
            sds((IMG, LEN, D), F32),
            sds((16, 2, 16, 256), BF16),
            sds((8, D), F32),
            sds((8, 2 * CH, D), BF16),
            sds((2, 2, 4, 128, CH), BF16),
            sds((4, 2, 4, 2, RA, CH), BF16),
            sds((4, 2, 2, 4, RB, CH), BF16),
            sds((4, 4, 4, RC, CH), BF16),
        ],
        scratch_shapes=[
            V((D, 2048), BF16),
            V((2, 2 * CH, D), BF16),
            V((2, 2, 4, 128, CH), BF16),
            V((ROWS, D), BF16),
            V((D, ROWS), BF16),
            V((ROWS, 3 * D), BF16),
            V((IMG * HEADS, PAD, PAD), BF16),
            V((ROWS, D), BF16),
            V((ROWS, D), F32),
            V((PAIR, D), BF16),
            V((PAIR, D), BF16),
            V((D, PAIR), BF16),
            V((D, PAIR), BF16),
            V((ROWS, 128), F32),
            V((PAIR, 128), BF16),
            V((PAIR, CH), BF16),
            V((PAIR, D), F32),
            V((PAIR, D), F32),
            V((PAIR, CH), F32),
            V((PAIR, 2 * CH), BF16),
            V((ROWS, D), BF16),
            V((ROWS, D), BF16),
            V((ROWS, 128), F32),
            V((ROWS, 128), F32),
            V((8, D), F32),
            V((8, D), F32),
            V((4, 4, 8, D), F32),
            V((ROWS, 128), BF16),
            V((8, 16, 128), BF16),
            V((128, D), BF16),
            V((4, 8, 32, 512), BF16),
            V((4, 2, 4, 32, 512), BF16),
            V((4, 4, 2, 16, 512), BF16),
            V((4, 2, 4, 16, 512), BF16),
            V((4, 2, 16, 512), BF16),
            V((4, 4, 16, 256), BF16),
            V((4, 16, 256), BF16),
            V((4, 16, 256), BF16),
            V((4, 2, 16, 512), BF16),
            V((2, 4, 16, 512), BF16),
            V((2, 16, 512), BF16),
            V((4, 16, 256), BF16),
            V((4, 2, 2, RA, CH), BF16),
            V((4, 4, RB, CH), BF16),
            V((4, 4, RC, CH), BF16),
            V((4, RA, CH), BF16),
            V((4, RB, CH), BF16),
            V((4, RC, CH), BF16),
            S((11,)),
            S((2, 2, 4)),
            S((2, 2, 2, 4)),
            S((2, 2, 2, 4)),
            S((2, 4)),
            S((2, 4)),
            S((2, 8)),
            S((2, 3, 4)),
            S((2, 2, 8)),
            S((2, 12)),
            S((2, 6)),
            S((2, 3)),
            S((3, 4)),
            S((4, 4)),
            S((2, 16, 4)),
            S((2, 4, 4)),
            S((2,)),
            S((2, 16)),
        ],
        compiler_params=pltpu.CompilerParams(
            collective_id=0, has_side_effects=True, vmem_limit_bytes=61 * 1024 * 1024
        ),
        cost_estimate=pl.CostEstimate(flops=50_000_000_000, bytes_accessed=60_000_000, transcendentals=10_000_000),
        name="layer",
    )(tokens, prep, cotangent, w_qkv, w_attn, v_in, w_in, w_out)
    sf, misc, f_all = outs[2], outs[3], outs[5]
    image = pl.BlockSpec((1, LEN, D), lambda e: (e, 0, 0))
    g_in, g_out, g_qkv, g_attn, layer_out, grad_tokens = pl.pallas_call(
        finish,
        grid=(4,),
        in_specs=[
            pl.BlockSpec((2, 2, D, 128), lambda e: (0, 0, 0, e)),
            pl.BlockSpec((16, 2, 16, 256), lambda e: (0, 0, 0, 0)),
            image,
            image,
        ],
        out_specs=[
            pl.BlockSpec((1, D, 256), lambda e: (e, 0, 0)),
            pl.BlockSpec((1, 256, D), lambda e: (e, 0, 0)),
            pl.BlockSpec((64, 3 * D), lambda e: (0, 0)),
            pl.BlockSpec((64, D), lambda e: (0, 0)),
            image,
            image,
        ],
        out_shape=[
            sds((4, D, 256), F32),
            sds((4, 256, D), F32),
            sds((64, 3 * D), F32),
            sds((64, D), F32),
            sds((IMG, LEN, D), BF16),
            sds((IMG, LEN, D), F32),
        ],
        name="finish",
    )(f_all.reshape(2, 2, D, CH), sf, outs[0], outs[1])
    mine = lax.dynamic_slice(misc, (0, 64 * lax.axis_index("fsdp")), (8, 64))
    return (layer_out, grad_tokens, mine[4], mine[5], g_qkv, g_attn, mine[6], mine[7], mine[:4].T, g_in, g_out)


def solution(mesh):
    dev = ("dp", "fsdp", "seq")
    in_specs = (
        P(dev, None, None), P(dev, None), P(dev), P(dev, None, None), P("fsdp"), P("fsdp"), P("fsdp", None),
        P("fsdp", None), P("fsdp"), P("fsdp"), P("fsdp", None), P(None, None, "fsdp"), P(None, "fsdp", None),
        P(dev, None, None),
    )
    out_specs = (
        P(dev, None, None), P(dev, None, None), P("fsdp"), P("fsdp"), P("fsdp", None), P("fsdp", None), P("fsdp"),
        P("fsdp"), P("fsdp", None), P(None, None, "fsdp"), P(None, "fsdp", None),
    )
    return jax.shard_map(per_device, mesh=mesh, in_specs=in_specs, out_specs=out_specs, check_vma=False)
```
